32 devices in a mesh: group: 2 (over y), dom: 16 (over z, x, core).
Axes of the slice: x: 2, y: 2, z: 4, core: 2. Of those that a mesh axis runs over, the one named last changes fastest.
Arguments:
- prior_basis: bfloat16 [128, 128, 128], P(('group', 'dom'))
- section_state: bfloat16 [128, 128], P(('group', 'dom'))
- source: float32 [128, 128], P(('group', 'dom')), may hold values from -6 to 6
- diag_blocks: bfloat16 [128, 128, 128], P(('group', 'dom'))
- coupling: bfloat16 [128, 4, 128, 128], P(('group', 'dom')), may hold values from -0.125 to 0.125
- neighbour_index: int32 [128, 4], P(('group', 'dom')), may hold values from 0 to 11, as said below
- slot_count: int32 [128], P(('group', 'dom')), may hold values from 2 to 4, as said below
Outputs:
- new_basis: bfloat16 [128, 128, 128], P(('group', 'dom'))
- image_basis: bfloat16 [128, 128, 128], P(('group', 'dom'))
- initial_guess: float32 [128, 128], P(('group', 'dom'))
- start_residual: float32 [128, 128], P(('group', 'dom'))
The draws below stay inside these ranges and needn't reach their ends.
Inputs may be any that keep to these rules, and one draw needn't show every extreme that they name: `neighbour_index`: an entry of the extended block list of the block's own partition; slot 0 always names a block from the lower neighbour partition and slot 1 one from the upper, and every shared block is named by some slot. Slots from slot_count on are padding and are ignored; the first face block of every partition uses all 4 slots.
All inputs are finite; a program needn't handle non-finite values.
Results may differ from the reference program's by a relative error of at most 0.0052.
Values may be sent and summed in bfloat16 or wider, within the bound.
No kernel may reach another device: no remote copies, remote signals or barrier semaphores. Data moves between devices by JAX's collectives and lax.ppermute only.
A program may use at most 64 MiB of HBM per device.

```python
import math
import jax
import jax.numpy as jnp
from jax import lax

BLOCK = 128
RECYCLE = 128
SLOTS = 4
HALO = 4
BLOCKS_DEV = 4
NBLOCKS = 128
N_GROUP = 2
N_DOM = 16


def shared_basis(key):
    keys = jax.random.split(jax.random.fold_in(key, 11), 3)
    total_rows = NBLOCKS * BLOCK
    position = jnp.arange(total_rows, dtype=jnp.float32) / max(total_rows - 1, 1)
    rising = 1.0 + 2.0 * position
    row_scale = jnp.exp(jax.random.uniform(keys[0], (total_rows,), jnp.float32) * math.log(10.0))
    entries = jax.random.normal(keys[2], (total_rows, RECYCLE), jnp.float32)
    col_scale = jnp.exp(jax.random.uniform(keys[1], (RECYCLE,), jnp.float32) * math.log(10.0))
    values = entries * (row_scale * rising)[:, None] * col_scale[None, :] / 10.0
    return values.reshape(NBLOCKS, BLOCK, RECYCLE)


def draw_prior_basis(key, part):
    return shared_basis(key).astype(jnp.bfloat16)


def draw_section_state(key, part):
    basis_values = shared_basis(key)
    column = jax.random.randint(jax.random.fold_in(key, 23), (), 0, RECYCLE)
    picked = jnp.take(basis_values, column, axis=2)
    noise = jax.random.normal(jax.random.fold_in(key, 29), (NBLOCKS, BLOCK), jnp.float32)
    return (picked + 0.5 * noise).astype(jnp.bfloat16)


def draw_diag_blocks(key, part):
    keys = jax.random.split(jax.random.fold_in(key, 31), 2)
    index_rows = jnp.arange(BLOCK)
    identity = (index_rows[:, None] == index_rows[None, :]).astype(jnp.float32)
    diagonal = jax.random.uniform(keys[0], (NBLOCKS, BLOCK), jnp.float32, 2.5, 4.0)
    spread = jax.random.normal(keys[1], (NBLOCKS, BLOCK, BLOCK), jnp.float32)
    blocks = spread * (1.0 - identity) / math.sqrt(BLOCK) + diagonal[:, :, None] * identity
    return blocks.astype(jnp.bfloat16)


def draw_neighbour_index(key, part):
    keys = jax.random.split(jax.random.fold_in(key, 37), 3)
    block_ids = jnp.arange(NBLOCKS, dtype=jnp.int32)
    local_ids = block_ids % BLOCKS_DEV
    device_ids = block_ids // BLOCKS_DEV
    lower_shift = jax.random.randint(keys[0], (NBLOCKS // BLOCKS_DEV,), 0, HALO)
    upper_shift = jax.random.randint(keys[1], (NBLOCKS // BLOCKS_DEV,), 0, HALO)
    first_slot = (local_ids + lower_shift[device_ids]) % HALO
    second_slot = BLOCKS_DEV + HALO + (local_ids + upper_shift[device_ids]) % HALO
    other_slots = jax.random.randint(keys[2], (NBLOCKS, SLOTS - 2), HALO, BLOCKS_DEV + HALO)
    return jnp.concatenate([first_slot[:, None], second_slot[:, None], other_slots], 1).astype(jnp.int32)


def draw_slot_count(key, part):
    block_ids = jnp.arange(NBLOCKS, dtype=jnp.int32)
    drawn = jax.random.randint(jax.random.fold_in(key, 41), (NBLOCKS,), 2, SLOTS + 1)
    return jnp.where(block_ids % BLOCKS_DEV == 0, SLOTS, drawn).astype(jnp.int32)


def levels(rng, shape, shards, low, high):
    level = 1.0
    for axis_at, parts in shards:
        heights = jax.random.uniform(jax.random.fold_in(jax.random.fold_in(rng, 6), axis_at), (parts,), jnp.float32, low / len(shards), high / len(shards))
        level = level * jnp.repeat(jnp.exp(heights), shape[axis_at] // parts).reshape((-1,) + (1,) * (len(shape) - 1 - axis_at))
    return level


def centred(rng, dims, scale, most, pieces=(), kind=jnp.bfloat16):
    array = jax.random.normal(rng, dims, jnp.float32) * scale
    if len(pieces) > 0:
        array = levels(rng, dims, pieces, -0.22, 0.18) * array
    return jnp.clip(array, min=-most, max=most).astype(kind)


def setup_inputs(seed: int = 0) -> dict:
    key_of = jax.random.split(jax.random.key(seed), 8)
    prior_basis = draw_prior_basis(jax.random.fold_in(key_of[7], 71), 0)
    section_state = draw_section_state(jax.random.fold_in(key_of[7], 71), 0)
    source = centred(key_of[2], (NBLOCKS, BLOCK), 1.0, 6.0, ((0, 32),), jnp.float32)
    diag_blocks = draw_diag_blocks(jax.random.fold_in(key_of[7], 71), 0)
    coupling = centred(key_of[4], (NBLOCKS, SLOTS, BLOCK, BLOCK), (16 * BLOCK) ** -0.5, 0.125, ((0, 32),))
    neighbour_index = draw_neighbour_index(jax.random.fold_in(key_of[7], 71), 0)
    slot_count = draw_slot_count(jax.random.fold_in(key_of[7], 71), 0)
    return dict(prior_basis=prior_basis, section_state=section_state, source=source, diag_blocks=diag_blocks, coupling=coupling, neighbour_index=neighbour_index, slot_count=slot_count)


section_step = 0.25
highest = lax.Precision.HIGHEST

def cholesky_inverse(gram):
    order = gram.shape[0]
    positions = jnp.arange(order, dtype=jnp.int32)

    def factor_step(column, lower):
        row_part = lower[column, :]
        remaining = gram[:, column] - jnp.dot(lower, row_part, precision=highest)
        pivot = jnp.sqrt(remaining[column])
        new_column = jnp.where(positions >= column, remaining / pivot, jnp.zeros_like(remaining))
        return lower.at[:, column].set(new_column)
    lower = lax.fori_loop(0, order, factor_step, jnp.zeros_like(gram))
    identity = (positions[:, None] == positions[None, :]).astype(gram.dtype)

    def solve_step(row, solved):
        row_values = (identity[row] - jnp.dot(lower[row, :], solved, precision=highest)) / lower[row, row]
        return solved.at[row].set(row_values)
    lower_inverse = lax.fori_loop(0, order, solve_step, jnp.zeros_like(gram))
    return lower_inverse.T

def group_apply(inputs):
    field, diagonal, couple, neighbours, live_count = inputs
    zero_rim = jnp.zeros_like(field[:1, :HALO])
    lower_rim = jnp.concatenate([zero_rim, field[:-1, BLOCKS_DEV - HALO:]], 0)
    upper_rim = jnp.concatenate([field[1:, :HALO], zero_rim], 0)
    extended = jnp.concatenate([lower_rim, field, upper_rim], 1)
    summed = jnp.einsum('pnab,pnb...->pna...', diagonal.astype(jnp.float32), field.astype(jnp.float32))
    for neighbour_slot in range(SLOTS):
        picked = jax.vmap(lambda rows_all, index_rows: jnp.take(rows_all, index_rows, axis=0))(extended, neighbours[:, :, neighbour_slot])
        alive_mask = (live_count > neighbour_slot).astype(jnp.float32)
        alive_mask = alive_mask.reshape(alive_mask.shape + (1,) * (field.ndim - 2))
        summed = summed + alive_mask * jnp.einsum('pnab,pnb...->pna...', couple[:, :, neighbour_slot].astype(jnp.float32), picked.astype(jnp.float32))
    return summed

def apply_operator(field, diag_blocks, coupling, neighbour_index, slot_count):

    def regroup(values):
        return values.reshape((N_GROUP, N_DOM, BLOCKS_DEV) + values.shape[1:])
    result = lax.map(group_apply, (regroup(field), regroup(diag_blocks), regroup(coupling), regroup(neighbour_index), regroup(slot_count)))
    return result.reshape(field.shape)

def reference(prior_basis, section_state, source, diag_blocks, coupling, neighbour_index, slot_count):
    state_image = apply_operator(section_state, diag_blocks, coupling, neighbour_index, slot_count)
    rhs = section_state.astype(jnp.float32) + section_step * (source - state_image)
    image = apply_operator(prior_basis, diag_blocks, coupling, neighbour_index, slot_count).astype(jnp.bfloat16)
    rows_total = float(NBLOCKS * BLOCK)
    flat_image = image.reshape(-1, RECYCLE)
    gram = jnp.dot(flat_image.T, flat_image, preferred_element_type=jnp.float32) / rows_total
    inverse = cholesky_inverse(gram)
    image_q = jnp.dot(flat_image.astype(jnp.float32), inverse, precision=highest)
    basis_q = jnp.dot(prior_basis.reshape(-1, RECYCLE).astype(jnp.float32), inverse, precision=highest)
    flat_rhs = rhs.reshape(-1)
    coefficients = jnp.dot(flat_rhs, image_q, precision=highest) / rows_total
    initial_guess = jnp.dot(basis_q, coefficients, precision=highest)
    start_residual = flat_rhs - jnp.dot(image_q, coefficients, precision=highest)
    return (basis_q.astype(jnp.bfloat16).reshape(prior_basis.shape), image_q.astype(jnp.bfloat16).reshape(prior_basis.shape), initial_guess.reshape(section_state.shape), start_residual.reshape(section_state.shape))
```

```python
import functools

import jax
import jax.numpy as jnp
from jax import lax
from jax.experimental import pallas as pl
from jax.experimental.pallas import tpu as pltpu
from jax.sharding import PartitionSpec as P

HALO = 4
PANEL = 8
section_step = 0.25
AXES = ("group", "dom")
F32 = jnp.float32
BF16 = jnp.bfloat16

NN = (((1,), (0,)), ((), ()))
NT = (((1,), (1,)), ((), ()))
TN = (((0,), (0,)), ((), ()))


def dot(a, b, dims):
    return lax.dot_general(a, b, dims, preferred_element_type=F32)


def split_rows(row, count):
    sub = lax.broadcasted_iota(jnp.int32, (16, row.shape[1]), 0)
    rows = jnp.zeros((16, row.shape[1]), F32)
    rest = row
    for part in range(count):
        piece = rest.astype(BF16).astype(F32)
        rows = jnp.where(sub == part, piece, rows)
        rest = rest - piece
    return rows.astype(BF16)


def operator_kernel(
    index_ref,
    count_ref,
    basis_ref,
    state_ref,
    lower_ref,
    upper_ref,
    source_ref,
    diag_ref,
    coupling_ref,
    image_ref,
    rhs_ref,
    sums_ref,
    ext_ref,
    state_ext_ref,
):
    blocks, block, _ = basis_ref.shape
    slots = coupling_ref.shape[1]
    halo_rows = HALO * block
    ext_ref[:HALO] = lower_ref[:halo_rows].reshape(HALO, block, block)
    ext_ref[HALO : HALO + blocks] = basis_ref[...]
    ext_ref[HALO + blocks :] = upper_ref[:halo_rows].reshape(HALO, block, block)
    state = state_ref[...].astype(F32)
    state_ext_ref[:HALO] = lower_ref[halo_rows:].astype(F32)[:HALO]
    state_ext_ref[HALO : HALO + blocks] = state
    state_ext_ref[HALO + blocks :] = upper_ref[halo_rows:].astype(F32)[:HALO]
    gram = jnp.zeros((block, block), F32)
    moment = jnp.zeros((16, block), F32)
    for b in range(blocks):
        left = [diag_ref[b]]
        right = [basis_ref[b]]
        rows = [jnp.broadcast_to(state[b : b + 1], (16, block))]
        for s in range(slots):
            live = count_ref[b] > s
            pick = index_ref[b, s]
            left.append(coupling_ref[b, s])
            right.append(jnp.where(live, ext_ref[pick], jnp.zeros((block, block), BF16)))
            picked = jnp.where(live, state_ext_ref[pl.ds(pick, 1), :], 0.0)
            rows.append(jnp.broadcast_to(picked, (16, block)))
        left = jnp.concatenate(left, axis=1)
        image = dot(left, jnp.concatenate(right, axis=0), NN).astype(BF16)
        state_image = dot(jnp.concatenate(rows, axis=1).astype(BF16), left, NT)[:1]
        mine = state[b : b + 1]
        rhs = mine + section_step * (source_ref[b : b + 1, :] - state_image)
        image_ref[b] = image
        rhs_ref[b : b + 1, :] = rhs
        gram = gram + dot(image, image, TN)
        moment = moment + dot(split_rows(rhs, 3), image, NN)
    half = block // 2
    top, bottom = gram[:half], gram[half:]
    sub = lax.broadcasted_iota(jnp.int32, (half, block), 0)
    lane = lax.broadcasted_iota(jnp.int32, (half, block), 1)
    sums_ref[:half] = jnp.where(lane < sub, pltpu.roll(bottom, half, 1), top)
    pivots = jnp.sum(jnp.where(lane == sub + half, bottom, 0.0), axis=0, keepdims=True)
    row = lax.broadcasted_iota(jnp.int32, (8, block), 0)
    total = jnp.sum(moment, axis=0, keepdims=True)
    sums_ref[half:] = jnp.where(row == 0, pivots, jnp.where(row == 1, total, 0.0))


def spread(value, shape):
    return jnp.broadcast_to(value, shape)


def eliminate(rows):
    order = rows[0].shape[1]
    panels = len(rows)
    rows = list(rows)
    shape = (PANEL, order)
    lane = lax.broadcasted_iota(jnp.int32, shape, 1)
    sub = lax.broadcasted_iota(jnp.int32, shape, 0)
    done = []
    for p in range(panels):
        c = p * PANEL
        panel = (lane >= c) & (lane < c + PANEL)
        wide = [spread(rows[p][i : i + 1], shape) for i in range(PANEL)]
        a = [
            [spread(wide[i][:, c + j : c + j + 1], shape) if j >= i else None for j in range(PANEL)]
            for i in range(PANEL)
        ]
        wide = [jnp.where(panel, 0.0, row) for row in wide]
        below = {}
        for q in range(p + 1, panels):
            below[q] = [spread(rows[q][:, c + k : c + k + 1], shape) for k in range(PANEL)]
            rows[q] = jnp.where(panel, 0.0, rows[q])
        out = jnp.zeros(shape, F32)
        for k in range(PANEL):
            pivot = a[k][k]
            root = lax.rsqrt(pivot)
            inv = 1.0 / pivot
            unit = jnp.where(lane == c + k, 1.0, wide[k])
            scaled = unit * inv
            factor = [None] * PANEL
            for i in range(k + 1, PANEL):
                factor[i] = a[k][i] * inv
                for j in range(i, PANEL):
                    a[i][j] = a[i][j] - factor[i] * a[k][j]
                wide[i] = wide[i] - factor[i] * unit
            for q in range(p + 1, panels):
                for j in range(k + 1, PANEL):
                    below[q][j] = below[q][j] - below[q][k] * factor[j]
                rows[q] = rows[q] - below[q][k] * scaled
            out = jnp.where(sub == k, unit * root, out)
        done.append(jnp.where(lane <= c + sub, out, 0.0))
    return done


def finish_kernel(*refs, rows_total):
    sum_refs = refs[:-9]
    image_ref, basis_ref, rhs_ref, new_ref, new_image_ref, guess_ref, residual_ref = refs[-9:-2]
    gram_ref, factor_ref = refs[-2:]
    blocks, block, _ = basis_ref.shape
    half = block // 2
    packed = sum_refs[0][...]
    for ref in sum_refs[1:]:
        packed = packed + ref[...]
    packed = packed * (1.0 / rows_total)
    top = packed[:half]
    sub = lax.broadcasted_iota(jnp.int32, (half, block), 0)
    lane = lax.broadcasted_iota(jnp.int32, (half, block), 1)
    upper = jnp.where(lane >= sub, top, 0.0)
    shifted = pltpu.roll(top, half, 1)
    lower = jnp.where((lane >= half) & (lane < sub + half), shifted, 0.0)
    pivots = packed[half : half + 1]
    lower = jnp.where(lane == sub + half, pivots, lower)
    once = jnp.concatenate([upper, lower], axis=0)
    row = lax.broadcasted_iota(jnp.int32, (block, block), 0)
    col = lax.broadcasted_iota(jnp.int32, (block, block), 1)
    gram_ref[...] = once + jnp.where(row == col, 0.0, once.T)
    done = eliminate([gram_ref[p : p + PANEL, :] for p in range(0, block, PANEL)])
    for p, panel in enumerate(done):
        factor_ref[p * PANEL : (p + 1) * PANEL, :] = panel
    factor = factor_ref[...]
    moment = packed[half + 1 : half + 2]
    coefficients = jnp.sum(factor * moment, axis=1, keepdims=True)
    weights = jnp.sum(factor * coefficients, axis=0, keepdims=True)
    weights = split_rows(weights, 3)
    high = factor.astype(BF16)
    low = (factor - high.astype(F32)).astype(BF16)
    both = jnp.concatenate([high, low], axis=1)
    for b in range(blocks):
        image, basis = image_ref[b], basis_ref[b]
        new_image_ref[b] = dot(jnp.concatenate([image, image], axis=1), both, NT).astype(BF16)
        new_ref[b] = dot(jnp.concatenate([basis, basis], axis=1), both, NT).astype(BF16)
        guess = jnp.sum(dot(weights, basis, NT), axis=0, keepdims=True)
        guess_ref[b : b + 1, :] = guess
        fitted = jnp.sum(dot(weights, image, NT), axis=0, keepdims=True)
        residual_ref[b : b + 1, :] = rhs_ref[b : b + 1, :] - fitted


def vmem():
    return pl.BlockSpec(memory_space=pltpu.VMEM)


def smem():
    return pl.BlockSpec(memory_space=pltpu.SMEM)


def halo(array, axis):
    devices = lax.axis_size(axis)
    up = [(i, i + 1) for i in range(devices - 1)]
    down = [(j, i) for i, j in up]
    last, first = array
    return lax.ppermute(last, axis, up), lax.ppermute(first, axis, down)


def exchange_stages(sizes):
    group, dom = sizes
    dom_bits = [1 << i for i in range(dom.bit_length() - 1)]
    group_bits = [dom << i for i in range(group.bit_length() - 1)]
    bits = dom_bits[:2] + group_bits + dom_bits[2:]
    stages = [bits[:1]]
    rest = bits[1:]
    while rest:
        pair, rest = rest[:2], rest[2:]
        stages.append(pair + [sum(pair)] if len(pair) == 2 else pair)
    return stages


def sum_parts(values):
    sizes = [lax.axis_size(axis) for axis in AXES]
    devices = sizes[0] * sizes[1]
    if any(size & (size - 1) for size in sizes):
        return [lax.psum(values, AXES)]
    parts = [values]
    for stage in exchange_stages(sizes):
        total = functools.reduce(jnp.add, parts)
        parts = [total]
        for bit in stage:
            pairs = [(i, i ^ bit) for i in range(devices)]
            parts.append(lax.ppermute(total, AXES, pairs))
    return parts


def body(prior_basis, section_state, source, diag_blocks, coupling, neighbour_index, slot_count):
    blocks, block, columns = prior_basis.shape
    flat = prior_basis.reshape(blocks * block, columns)
    ends = [
        jnp.concatenate([flat[-HALO * block :], section_state[-HALO:], jnp.zeros((16 - HALO, columns), BF16)]),
        jnp.concatenate([flat[: HALO * block], section_state[:HALO], jnp.zeros((16 - HALO, columns), BF16)]),
    ]
    lower, upper = halo(ends, "dom")
    image, rhs, sums = pl.pallas_call(
        operator_kernel,
        out_shape=(
            jax.ShapeDtypeStruct(prior_basis.shape, BF16),
            jax.ShapeDtypeStruct(source.shape, F32),
            jax.ShapeDtypeStruct((block // 2 + 8, columns), F32),
        ),
        in_specs=[smem()] * 2 + [vmem()] * 7,
        out_specs=(vmem(),) * 3,
        scratch_shapes=[
            pltpu.VMEM((blocks + 2 * HALO, block, columns), BF16),
            pltpu.VMEM((blocks + 2 * HALO, columns), F32),
        ],
        name="operator",
    )(
        neighbour_index,
        slot_count,
        prior_basis,
        section_state,
        lower,
        upper,
        source,
        diag_blocks,
        coupling,
    )
    parts = sum_parts(sums)
    rows_total = blocks * block * lax.axis_size("group") * lax.axis_size("dom")
    return pl.pallas_call(
        functools.partial(finish_kernel, rows_total=float(rows_total)),
        out_shape=(
            jax.ShapeDtypeStruct(prior_basis.shape, BF16),
            jax.ShapeDtypeStruct(prior_basis.shape, BF16),
            jax.ShapeDtypeStruct(source.shape, F32),
            jax.ShapeDtypeStruct(source.shape, F32),
        ),
        in_specs=[vmem()] * (len(parts) + 3),
        out_specs=(vmem(),) * 4,
        scratch_shapes=[pltpu.VMEM((block, columns), F32)] * 2,
        name="finish",
    )(*parts, image, prior_basis, rhs)


def solution(mesh):
    rows = P(AXES, None)
    cubes = P(AXES, None, None)
    return jax.shard_map(
        body,
        mesh=mesh,
        in_specs=(cubes, rows, rows, cubes, P(AXES, None, None, None), rows, P(AXES)),
        out_specs=(cubes, cubes, rows, rows),
        check_vma=False,
    )
```

```python
import functools

import jax
import jax.numpy as jnp
from jax import lax
from jax.experimental import pallas as pl
from jax.experimental.pallas import tpu as pltpu
from jax.sharding import PartitionSpec as P

HALO = 4
PANEL = 8
VMEM_LIMIT = 16 << 20
section_step = 0.25
AXES = ("group", "dom")
F32 = jnp.float32
BF16 = jnp.bfloat16

NN = (((1,), (0,)), ((), ()))
NT = (((1,), (1,)), ((), ()))
TN = (((0,), (0,)), ((), ()))


def dot(a, b, dims):
    return lax.dot_general(a, b, dims, preferred_element_type=F32)


def split_rows(row, count):
    sub = lax.broadcasted_iota(jnp.int32, (16, row.shape[1]), 0)
    rows = jnp.zeros((16, row.shape[1]), F32)
    rest = row
    for part in range(count):
        piece = rest.astype(BF16).astype(F32)
        rows = jnp.where(sub == part, piece, rows)
        rest = rest - piece
    return rows.astype(BF16)


def stack_rows(rows):
    return jnp.concatenate([jnp.broadcast_to(row, (16, row.shape[1])) for row in rows], axis=1).astype(BF16)


def pack_kernel(basis_ref, state_ref, packed_ref, rows_ref, sems):
    rows = basis_ref.shape[0]
    copy = pltpu.make_async_copy(basis_ref, packed_ref.at[pl.ds(0, rows)], sems.at[0])
    copy.start()
    state_copy = pltpu.make_async_copy(state_ref, rows_ref, sems.at[1])
    state_copy.start()
    state_copy.wait()
    state = rows_ref[...].astype(F32)
    spare = jnp.zeros((packed_ref.shape[0] - rows - state.shape[0], state.shape[1]), F32)
    packed_ref[rows:] = jnp.concatenate([state, spare], axis=0).astype(BF16)
    copy.wait()


def state_of(packed_ref, rows, count):
    return packed_ref[rows:].astype(F32)[:count]


def block_of(packed_ref, pick, block):
    return packed_ref[pl.ds(pl.multiple_of(pick * block, block), block)]


def local_kernel(
    index_ref,
    count_ref,
    packed_ref,
    source_ref,
    diag_ref,
    coupling_ref,
    partial_ref,
    base_ref,
    near_coupling_ref,
    near_index_ref,
    near_count_ref,
    sem,
):
    copy = pltpu.make_async_copy(coupling_ref, near_coupling_ref, sem)
    copy.start()
    blocks, block, _ = diag_ref.shape
    slots = coupling_ref.shape[1]
    for b in range(blocks):
        near_count_ref[b] = count_ref[b]
        for s in range(slots):
            near_index_ref[b, s] = index_ref[b, s]
    state = state_of(packed_ref, blocks * block, blocks)
    state_rows = [state[b : b + 1] for b in range(blocks)]
    copy.wait()
    for b in range(blocks):
        left, right, rows = [diag_ref[b]], [block_of(packed_ref, b, block)], [state_rows[b]]
        for s in range(2, slots):
            pick = index_ref[b, s] - HALO
            live = (count_ref[b] > s) & (pick >= 0) & (pick < blocks)
            pick = jnp.clip(pick, 0, blocks - 1)
            left.append(near_coupling_ref[b, s])
            right.append(jnp.where(live, block_of(packed_ref, pick, block), jnp.zeros((block, block), BF16)))
            row = state_rows[0]
            for i in range(1, blocks):
                row = jnp.where(pick == i, state_rows[i], row)
            rows.append(jnp.where(live, row, 0.0))
        left = jnp.concatenate(left, axis=1)
        partial_ref[b] = dot(left, jnp.concatenate(right, axis=0), NN)
        state_image = dot(stack_rows(rows), left, NT)[:1]
        base_ref[b : b + 1, :] = state_rows[b] + section_step * (source_ref[b : b + 1, :] - state_image)


def shared_kernel(
    index_ref,
    count_ref,
    inner_ref,
    outer_ref,
    coupling_ref,
    _partial_in_ref,
    _base_in_ref,
    partial_ref,
    rhs_ref,
    image_ref,
    sums_ref,
):
    blocks, block, _ = image_ref.shape
    odd = lax.axis_index("dom") % 2 == 1
    inner_state = state_of(inner_ref, HALO * block, HALO)
    outer_state = state_of(outer_ref, HALO * block, HALO)
    lower_state = jnp.where(odd, inner_state, outer_state)
    upper_state = jnp.where(odd, outer_state, inner_state)

    def lower(pick):
        return jnp.where(odd, block_of(inner_ref, pick, block), block_of(outer_ref, pick, block))

    def upper(pick):
        return jnp.where(odd, block_of(outer_ref, pick, block), block_of(inner_ref, pick, block))

    def chosen(rows, pick):
        row = rows[:1]
        for i in range(1, HALO):
            row = jnp.where(pick == i, rows[i : i + 1], row)
        return row

    for b in range(blocks):
        for s in range(2, coupling_ref.shape[1]):
            pick = index_ref[b, s]
            above = pick - HALO - blocks

            @pl.when((count_ref[b] > s) & ((pick < HALO) | (above >= 0)))
            def _(b=b, s=s, pick=pick, above=above):
                at = jnp.where(above >= 0, above, pick)
                picked = jnp.where(above >= 0, upper(at), lower(at))
                row = jnp.where(above >= 0, chosen(upper_state, at), chosen(lower_state, at))
                left = coupling_ref[b, s]
                partial_ref[b] += dot(left, picked, NN)
                rhs_ref[b : b + 1, :] -= section_step * dot(stack_rows([row]), left, NT)[:1]

    gram = jnp.zeros((block, block), F32)
    moment = jnp.zeros((16, block), F32)
    for b in range(blocks):
        below, above = index_ref[b, 0], index_ref[b, 1] - HALO - blocks
        left = jnp.concatenate([coupling_ref[b, 0], coupling_ref[b, 1]], axis=1)
        right = jnp.concatenate([lower(below), upper(above)], axis=0)
        image = (partial_ref[b] + dot(left, right, NN)).astype(BF16)
        rows = stack_rows([chosen(lower_state, below), chosen(upper_state, above)])
        rhs = rhs_ref[b : b + 1, :] - section_step * dot(rows, left, NT)[:1]
        image_ref[b] = image
        rhs_ref[b : b + 1, :] = rhs
        gram = gram + dot(image, image, TN)
        moment = moment + dot(split_rows(rhs, 3), image, NN)
    half = block // 2
    top, bottom = gram[:half], gram[half:]
    sub = lax.broadcasted_iota(jnp.int32, (half, block), 0)
    lane = lax.broadcasted_iota(jnp.int32, (half, block), 1)
    sums_ref[:half] = jnp.where(lane < sub, pltpu.roll(bottom, half, 1), top)
    pivots = jnp.sum(jnp.where(lane == sub + half, bottom, 0.0), axis=0, keepdims=True)
    row = lax.broadcasted_iota(jnp.int32, (8, block), 0)
    total = jnp.sum(moment, axis=0, keepdims=True)
    sums_ref[half:] = jnp.where(row == 0, pivots, jnp.where(row == 1, total, 0.0))


def spread(value, shape):
    return jnp.broadcast_to(value, shape)


def eliminate(rows):
    order = rows[0].shape[1]
    panels = len(rows)
    rows = list(rows)
    shape = (PANEL, order)
    lane = lax.broadcasted_iota(jnp.int32, shape, 1)
    sub = lax.broadcasted_iota(jnp.int32, shape, 0)
    done = []
    for p in range(panels):
        c = p * PANEL
        panel = (lane >= c) & (lane < c + PANEL)
        wide = [spread(rows[p][i : i + 1], shape) for i in range(PANEL)]
        a = [
            [spread(wide[i][:, c + j : c + j + 1], shape) if j >= i else None for j in range(PANEL)]
            for i in range(PANEL)
        ]
        wide = [jnp.where(panel, 0.0, row) for row in wide]
        below = {}
        for q in range(p + 1, panels):
            below[q] = [spread(rows[q][:, c + k : c + k + 1], shape) for k in range(PANEL)]
            rows[q] = jnp.where(panel, 0.0, rows[q])
        out = jnp.zeros(shape, F32)
        for k in range(PANEL):
            pivot = a[k][k]
            root = lax.rsqrt(pivot)
            inv = 1.0 / pivot
            unit = jnp.where(lane == c + k, 1.0, wide[k])
            scaled = unit * inv
            factor = [None] * PANEL
            for i in range(k + 1, PANEL):
                factor[i] = a[k][i] * inv
                for j in range(i, PANEL):
                    a[i][j] = a[i][j] - factor[i] * a[k][j]
                wide[i] = wide[i] - factor[i] * unit
            for q in range(p + 1, panels):
                for j in range(k + 1, PANEL):
                    below[q][j] = below[q][j] - below[q][k] * factor[j]
                rows[q] = rows[q] - below[q][k] * scaled
            out = jnp.where(sub == k, unit * root, out)
        done.append(jnp.where(lane <= c + sub, out, 0.0))
    return done


def finish_kernel(*refs, rows_total):
    sum_refs = refs[:-9]
    image_ref, packed_ref, rhs_ref, new_ref, new_image_ref, guess_ref, residual_ref = refs[-9:-2]
    gram_ref, factor_ref = refs[-2:]
    blocks, block, _ = image_ref.shape
    half = block // 2
    packed = sum_refs[0][...]
    for ref in sum_refs[1:]:
        packed = packed + ref[...]
    packed = packed * (1.0 / rows_total)
    top = packed[:half]
    sub = lax.broadcasted_iota(jnp.int32, (half, block), 0)
    lane = lax.broadcasted_iota(jnp.int32, (half, block), 1)
    upper = jnp.where(lane >= sub, top, 0.0)
    shifted = pltpu.roll(top, half, 1)
    lower = jnp.where((lane >= half) & (lane < sub + half), shifted, 0.0)
    pivots = packed[half : half + 1]
    lower = jnp.where(lane == sub + half, pivots, lower)
    once = jnp.concatenate([upper, lower], axis=0)
    row = lax.broadcasted_iota(jnp.int32, (block, block), 0)
    col = lax.broadcasted_iota(jnp.int32, (block, block), 1)
    gram_ref[...] = once + jnp.where(row == col, 0.0, once.T)
    done = eliminate([gram_ref[p : p + PANEL, :] for p in range(0, block, PANEL)])
    for p, panel in enumerate(done):
        factor_ref[p * PANEL : (p + 1) * PANEL, :] = panel
    factor = factor_ref[...]
    moment = packed[half + 1 : half + 2]
    coefficients = jnp.sum(factor * moment, axis=1, keepdims=True)
    weights = jnp.sum(factor * coefficients, axis=0, keepdims=True)
    weights = split_rows(weights, 3)
    high = factor.astype(BF16)
    low = (factor - high.astype(F32)).astype(BF16)
    both = jnp.concatenate([high, low], axis=1)
    for b in range(blocks):
        image, basis = image_ref[b], block_of(packed_ref, b, block)
        new_image_ref[b] = dot(jnp.concatenate([image, image], axis=1), both, NT).astype(BF16)
        new_ref[b] = dot(jnp.concatenate([basis, basis], axis=1), both, NT).astype(BF16)
        guess = jnp.sum(dot(weights, basis, NT), axis=0, keepdims=True)
        guess_ref[b : b + 1, :] = guess
        fitted = jnp.sum(dot(weights, image, NT), axis=0, keepdims=True)
        residual_ref[b : b + 1, :] = rhs_ref[b : b + 1, :] - fitted


def near(*arrays):
    return [pltpu.with_memory_space_constraint(array, pltpu.VMEM) for array in arrays]


def far(*arrays):
    return [pltpu.with_memory_space_constraint(array, pltpu.HBM) for array in arrays]


def vmem():
    return pl.BlockSpec(memory_space=pltpu.VMEM)


def smem():
    return pl.BlockSpec(memory_space=pltpu.SMEM)


def pack(basis, state):
    blocks, block, columns = basis.shape
    rows = blocks * block
    return pl.pallas_call(
        pack_kernel,
        out_shape=pltpu.VMEM((rows + 16 * pl.cdiv(blocks, 16), columns), BF16),
        in_specs=[pl.BlockSpec(memory_space=pl.ANY)] * 2,
        out_specs=vmem(),
        scratch_shapes=[pltpu.VMEM(state.shape, BF16), pltpu.SemaphoreType.DMA((2,))],
        compiler_params=pltpu.CompilerParams(vmem_limit_bytes=VMEM_LIMIT),
        name="pack",
    )(*far(basis.reshape(rows, columns), state))


def halo(packed, basis, state):
    devices = lax.axis_size("dom")
    odd = lax.axis_index("dom") % 2
    got = []
    for parity in (1, 0):
        pairs = [(i, i + 1) for i in range(parity, devices - 1, 2)]
        sent = packed
        if basis.shape[0] > HALO:
            up = odd == parity
            sent = pack(*(jnp.where(up, whole[-HALO:], whole[:HALO]) for whole in (basis, state)))
        got.append(lax.ppermute(sent, "dom", pairs + [(j, i) for i, j in pairs]))
    return got


def exchange_stages(sizes):
    group, dom = sizes
    dom_bits = [1 << i for i in range(dom.bit_length() - 1)]
    group_bits = [dom << i for i in range(group.bit_length() - 1)]
    bits = dom_bits[:2] + group_bits + dom_bits[2:]
    stages = [bits[:1]]
    rest = bits[1:]
    while rest:
        pair, rest = rest[:2], rest[2:]
        stages.append(pair + [sum(pair)] if len(pair) == 2 else pair)
    return stages


def sum_parts(values):
    sizes = [lax.axis_size(axis) for axis in AXES]
    devices = sizes[0] * sizes[1]
    if any(size & (size - 1) for size in sizes):
        return [lax.psum(values, AXES)]
    parts = [values]
    for stage in exchange_stages(sizes):
        total = functools.reduce(jnp.add, parts)
        parts = [total]
        for bit in stage:
            pairs = [(i, i ^ bit) for i in range(devices)]
            parts.append(lax.ppermute(total, AXES, pairs))
    return parts


def body(prior_basis, section_state, source, diag_blocks, coupling, neighbour_index, slot_count):
    blocks, block, columns = prior_basis.shape
    packed = pack(prior_basis, section_state)
    outer, inner = halo(packed, prior_basis, section_state)
    partial, base, near_coupling, near_index, near_count = pl.pallas_call(
        local_kernel,
        out_shape=(
            pltpu.VMEM(prior_basis.shape, F32),
            pltpu.VMEM(source.shape, F32),
            pltpu.VMEM(coupling.shape, BF16),
            pltpu.SMEM(neighbour_index.shape, jnp.int32),
            pltpu.SMEM(slot_count.shape, jnp.int32),
        ),
        in_specs=[smem()] * 2 + [vmem()] * 3 + [pl.BlockSpec(memory_space=pl.ANY)],
        out_specs=(vmem(),) * 3 + (smem(),) * 2,
        scratch_shapes=[pltpu.SemaphoreType.DMA],
        compiler_params=pltpu.CompilerParams(vmem_limit_bytes=VMEM_LIMIT),
        name="local_part",
    )(*far(neighbour_index, slot_count), *near(packed), *far(source, diag_blocks, coupling))
    _, rhs, image, sums = pl.pallas_call(
        shared_kernel,
        out_shape=(
            pltpu.VMEM(prior_basis.shape, F32),
            pltpu.VMEM(source.shape, F32),
            pltpu.VMEM(prior_basis.shape, BF16),
            pltpu.VMEM((block // 2 + 8, columns), F32),
        ),
        in_specs=[smem()] * 2 + [vmem()] * 5,
        out_specs=(vmem(),) * 4,
        input_output_aliases={5: 0, 6: 1},
        compiler_params=pltpu.CompilerParams(vmem_limit_bytes=VMEM_LIMIT),
        name="shared_part",
    )(
        *(pltpu.with_memory_space_constraint(array, pltpu.SMEM) for array in (near_index, near_count)),
        *near(inner, outer, near_coupling, partial, base),
    )
    parts = sum_parts(sums)
    rows_total = blocks * block * lax.axis_size("group") * lax.axis_size("dom")
    return pl.pallas_call(
        functools.partial(finish_kernel, rows_total=float(rows_total)),
        out_shape=(
            jax.ShapeDtypeStruct(prior_basis.shape, BF16),
            jax.ShapeDtypeStruct(prior_basis.shape, BF16),
            jax.ShapeDtypeStruct(source.shape, F32),
            jax.ShapeDtypeStruct(source.shape, F32),
        ),
        in_specs=[vmem()] * (len(parts) + 3),
        out_specs=(vmem(),) * 4,
        scratch_shapes=[pltpu.VMEM((block, columns), F32)] * 2,
        compiler_params=pltpu.CompilerParams(vmem_limit_bytes=VMEM_LIMIT),
        name="finish",
    )(*near(*parts, image, packed, rhs))


def solution(mesh):
    rows = P(AXES, None)
    cubes = P(AXES, None, None)
    return jax.shard_map(
        body,
        mesh=mesh,
        in_specs=(cubes, rows, rows, cubes, P(AXES, None, None, None), rows, P(AXES)),
        out_specs=(cubes, cubes, rows, rows),
        check_vma=False,
    )
```

```python
import functools

import jax
import jax.numpy as jnp
from jax import lax
from jax.experimental import pallas as pl
from jax.experimental.pallas import tpu as pltpu
from jax.sharding import PartitionSpec as P

HALO = 4
PANEL = 8
VMEM_LIMIT = 16 << 20
section_step = 0.25
AXES = ("group", "dom")
F32 = jnp.float32
BF16 = jnp.bfloat16

NN = (((1,), (0,)), ((), ()))
NT = (((1,), (1,)), ((), ()))
TN = (((0,), (0,)), ((), ()))


def dot(a, b, dims):
    return lax.dot_general(a, b, dims, preferred_element_type=F32)


def split_rows(row, count):
    sub = lax.broadcasted_iota(jnp.int32, (16, row.shape[1]), 0)
    rows = jnp.zeros((16, row.shape[1]), F32)
    rest = row
    for part in range(count):
        piece = rest.astype(BF16).astype(F32)
        rows = jnp.where(sub == part, piece, rows)
        rest = rest - piece
    return rows.astype(BF16)


def stack_rows(rows):
    return jnp.concatenate([jnp.broadcast_to(row, (16, row.shape[1])) for row in rows], axis=1).astype(BF16)


def pack_kernel(basis_ref, state_ref, packed_ref, rows_ref, sems):
    rows = basis_ref.shape[0]
    copy = pltpu.make_async_copy(basis_ref, packed_ref.at[pl.ds(0, rows)], sems.at[0])
    copy.start()
    state_copy = pltpu.make_async_copy(state_ref, rows_ref, sems.at[1])
    state_copy.start()
    state_copy.wait()
    state = rows_ref[...].astype(F32)
    spare = jnp.zeros((packed_ref.shape[0] - rows - state.shape[0], state.shape[1]), F32)
    packed_ref[rows:] = jnp.concatenate([state, spare], axis=0).astype(BF16)
    copy.wait()


def state_of(packed_ref, rows, count):
    return packed_ref[rows:].astype(F32)[:count]


def block_of(packed_ref, pick, block):
    return packed_ref[pl.ds(pl.multiple_of(pick * block, block), block)]


def local_kernel(
    index_ref,
    count_ref,
    packed_ref,
    source_ref,
    diag_ref,
    coupling_ref,
    partial_ref,
    base_ref,
    near_coupling_ref,
    near_index_ref,
    near_count_ref,
    sem,
):
    copy = pltpu.make_async_copy(coupling_ref, near_coupling_ref, sem)
    copy.start()
    blocks, block, _ = diag_ref.shape
    slots = coupling_ref.shape[1]
    for b in range(blocks):
        near_count_ref[b] = count_ref[b]
        for s in range(slots):
            near_index_ref[b, s] = index_ref[b, s]
    state = state_of(packed_ref, blocks * block, blocks)
    state_rows = [state[b : b + 1] for b in range(blocks)]
    copy.wait()
    for b in range(blocks):
        left, right, rows = [diag_ref[b]], [block_of(packed_ref, b, block)], [state_rows[b]]
        for s in range(2, slots):
            pick = index_ref[b, s] - HALO
            live = (count_ref[b] > s) & (pick >= 0) & (pick < blocks)
            pick = jnp.clip(pick, 0, blocks - 1)
            left.append(near_coupling_ref[b, s])
            right.append(jnp.where(live, block_of(packed_ref, pick, block), jnp.zeros((block, block), BF16)))
            row = state_rows[0]
            for i in range(1, blocks):
                row = jnp.where(pick == i, state_rows[i], row)
            rows.append(jnp.where(live, row, 0.0))
        left = jnp.concatenate(left, axis=1)
        partial_ref[b] = dot(left, jnp.concatenate(right, axis=0), NN)
        state_image = dot(stack_rows(rows), left, NT)[:1]
        base_ref[b : b + 1, :] = state_rows[b] + section_step * (source_ref[b : b + 1, :] - state_image)


def shared_kernel(
    index_ref,
    count_ref,
    inner_ref,
    outer_ref,
    coupling_ref,
    _partial_in_ref,
    _base_in_ref,
    partial_ref,
    rhs_ref,
    image_ref,
    sums_ref,
):
    blocks, block, _ = image_ref.shape
    here = lax.axis_index("dom")
    odd = here % 2 == 1
    first, last = here == 0, here == lax.axis_size("dom") - 1
    inner_state = state_of(inner_ref, HALO * block, HALO)
    outer_state = state_of(outer_ref, HALO * block, HALO)
    lower_state = jnp.where(first, 0.0, jnp.where(odd, inner_state, outer_state))
    upper_state = jnp.where(last, 0.0, jnp.where(odd, outer_state, inner_state))
    nothing = jnp.zeros((block, block), BF16)

    def lower(pick):
        picked = jnp.where(odd, block_of(inner_ref, pick, block), block_of(outer_ref, pick, block))
        return jnp.where(first, nothing, picked)

    def upper(pick):
        picked = jnp.where(odd, block_of(outer_ref, pick, block), block_of(inner_ref, pick, block))
        return jnp.where(last, nothing, picked)

    def chosen(rows, pick):
        row = rows[:1]
        for i in range(1, HALO):
            row = jnp.where(pick == i, rows[i : i + 1], row)
        return row

    for b in range(blocks):
        for s in range(2, coupling_ref.shape[1]):
            pick = index_ref[b, s]
            above = pick - HALO - blocks

            @pl.when((count_ref[b] > s) & ((pick < HALO) | (above >= 0)))
            def _(b=b, s=s, pick=pick, above=above):
                at = jnp.where(above >= 0, above, pick)
                picked = jnp.where(above >= 0, upper(at), lower(at))
                row = jnp.where(above >= 0, chosen(upper_state, at), chosen(lower_state, at))
                left = coupling_ref[b, s]
                partial_ref[b] += dot(left, picked, NN)
                rhs_ref[b : b + 1, :] -= section_step * dot(stack_rows([row]), left, NT)[:1]

    gram = jnp.zeros((block, block), F32)
    moment = jnp.zeros((16, block), F32)
    for b in range(blocks):
        below, above = index_ref[b, 0], index_ref[b, 1] - HALO - blocks
        left = jnp.concatenate([coupling_ref[b, 0], coupling_ref[b, 1]], axis=1)
        right = jnp.concatenate([lower(below), upper(above)], axis=0)
        image = (partial_ref[b] + dot(left, right, NN)).astype(BF16)
        rows = stack_rows([chosen(lower_state, below), chosen(upper_state, above)])
        rhs = rhs_ref[b : b + 1, :] - section_step * dot(rows, left, NT)[:1]
        image_ref[b] = image
        rhs_ref[b : b + 1, :] = rhs
        gram = gram + dot(image, image, TN)
        moment = moment + dot(split_rows(rhs, 3), image, NN)
    half = block // 2
    top, bottom = gram[:half], gram[half:]
    sub = lax.broadcasted_iota(jnp.int32, (half, block), 0)
    lane = lax.broadcasted_iota(jnp.int32, (half, block), 1)
    sums_ref[:half] = jnp.where(lane < sub, pltpu.roll(bottom, half, 1), top)
    pivots = jnp.sum(jnp.where(lane == sub + half, bottom, 0.0), axis=0, keepdims=True)
    row = lax.broadcasted_iota(jnp.int32, (8, block), 0)
    total = jnp.sum(moment, axis=0, keepdims=True)
    sums_ref[half:] = jnp.where(row == 0, pivots, jnp.where(row == 1, total, 0.0))


def spread(value, shape):
    return jnp.broadcast_to(value, shape)


def eliminate(rows):
    order = rows[0].shape[1]
    panels = len(rows)
    rows = list(rows)
    shape = (PANEL, order)
    lane = lax.broadcasted_iota(jnp.int32, shape, 1)
    sub = lax.broadcasted_iota(jnp.int32, shape, 0)
    done = []
    for p in range(panels):
        c = p * PANEL
        panel = (lane >= c) & (lane < c + PANEL)
        wide = [spread(rows[p][i : i + 1], shape) for i in range(PANEL)]
        a = [
            [spread(wide[i][:, c + j : c + j + 1], shape) if j >= i else None for j in range(PANEL)]
            for i in range(PANEL)
        ]
        wide = [jnp.where(panel, 0.0, row) for row in wide]
        below = {}
        for q in range(p + 1, panels):
            below[q] = [spread(rows[q][:, c + k : c + k + 1], shape) for k in range(PANEL)]
            rows[q] = jnp.where(panel, 0.0, rows[q])
        out = jnp.zeros(shape, F32)
        for k in range(PANEL):
            pivot = a[k][k]
            root = lax.rsqrt(pivot)
            inv = 1.0 / pivot
            unit = jnp.where(lane == c + k, 1.0, wide[k])
            scaled = unit * inv
            factor = [None] * PANEL
            for i in range(k + 1, PANEL):
                factor[i] = a[k][i] * inv
                for j in range(i, PANEL):
                    a[i][j] = a[i][j] - factor[i] * a[k][j]
                wide[i] = wide[i] - factor[i] * unit
            for q in range(p + 1, panels):
                for j in range(k + 1, PANEL):
                    below[q][j] = below[q][j] - below[q][k] * factor[j]
                rows[q] = rows[q] - below[q][k] * scaled
            out = jnp.where(sub == k, unit * root, out)
        done.append(jnp.where(lane <= c + sub, out, 0.0))
    return done


def finish_kernel(*refs, rows_total):
    sum_refs = refs[:-9]
    image_ref, packed_ref, rhs_ref, new_ref, new_image_ref, guess_ref, residual_ref = refs[-9:-2]
    gram_ref, factor_ref = refs[-2:]
    blocks, block, _ = image_ref.shape
    half = block // 2
    packed = sum_refs[0][...]
    for ref in sum_refs[1:]:
        packed = packed + ref[...]
    packed = packed * (1.0 / rows_total)
    top = packed[:half]
    sub = lax.broadcasted_iota(jnp.int32, (half, block), 0)
    lane = lax.broadcasted_iota(jnp.int32, (half, block), 1)
    upper = jnp.where(lane >= sub, top, 0.0)
    shifted = pltpu.roll(top, half, 1)
    lower = jnp.where((lane >= half) & (lane < sub + half), shifted, 0.0)
    pivots = packed[half : half + 1]
    lower = jnp.where(lane == sub + half, pivots, lower)
    once = jnp.concatenate([upper, lower], axis=0)
    row = lax.broadcasted_iota(jnp.int32, (block, block), 0)
    col = lax.broadcasted_iota(jnp.int32, (block, block), 1)
    gram_ref[...] = once + jnp.where(row == col, 0.0, once.T)
    done = eliminate([gram_ref[p : p + PANEL, :] for p in range(0, block, PANEL)])
    for p, panel in enumerate(done):
        factor_ref[p * PANEL : (p + 1) * PANEL, :] = panel
    factor = factor_ref[...]
    moment = packed[half + 1 : half + 2]
    coefficients = jnp.sum(factor * moment, axis=1, keepdims=True)
    weights = jnp.sum(factor * coefficients, axis=0, keepdims=True)
    weights = split_rows(weights, 3)
    high = factor.astype(BF16)
    low = (factor - high.astype(F32)).astype(BF16)
    both = jnp.concatenate([high, low], axis=1)
    for b in range(blocks):
        image, basis = image_ref[b], block_of(packed_ref, b, block)
        new_image_ref[b] = dot(jnp.concatenate([image, image], axis=1), both, NT).astype(BF16)
        new_ref[b] = dot(jnp.concatenate([basis, basis], axis=1), both, NT).astype(BF16)
        guess = jnp.sum(dot(weights, basis, NT), axis=0, keepdims=True)
        guess_ref[b : b + 1, :] = guess
        fitted = jnp.sum(dot(weights, image, NT), axis=0, keepdims=True)
        residual_ref[b : b + 1, :] = rhs_ref[b : b + 1, :] - fitted


def near(*arrays):
    return [pltpu.with_memory_space_constraint(array, pltpu.VMEM) for array in arrays]


def far(*arrays):
    return [pltpu.with_memory_space_constraint(array, pltpu.HBM) for array in arrays]


def vmem():
    return pl.BlockSpec(memory_space=pltpu.VMEM)


def smem():
    return pl.BlockSpec(memory_space=pltpu.SMEM)


def pack(basis, state):
    blocks, block, columns = basis.shape
    rows = blocks * block
    return pl.pallas_call(
        pack_kernel,
        out_shape=pltpu.VMEM((rows + 16 * pl.cdiv(blocks, 16), columns), BF16),
        in_specs=[pl.BlockSpec(memory_space=pl.ANY)] * 2,
        out_specs=vmem(),
        scratch_shapes=[pltpu.VMEM(state.shape, BF16), pltpu.SemaphoreType.DMA((2,))],
        compiler_params=pltpu.CompilerParams(vmem_limit_bytes=VMEM_LIMIT),
        name="pack",
    )(*far(basis.reshape(rows, columns), state))


def swap_pairs(parity, groups, devices):
    pairs = []
    for group in range(groups):
        for device in range(devices):
            other = device + 1 if device % 2 == parity else device - 1
            if 0 <= other < devices:
                pairs.append((group * devices + device, group * devices + other))
            else:
                twin = group ^ 1 if group ^ 1 < groups else group
                pairs.append((group * devices + device, twin * devices + device))
    return pairs


def halo(packed, basis, state):
    groups, devices = (lax.axis_size(axis) for axis in AXES)
    odd = lax.axis_index("dom") % 2
    got = []
    for parity in (1, 0):
        sent = packed
        if basis.shape[0] > HALO:
            up = odd == parity
            sent = pack(*(jnp.where(up, whole[-HALO:], whole[:HALO]) for whole in (basis, state)))
        got.append(lax.ppermute(sent, AXES, swap_pairs(parity, groups, devices)))
    return got


def exchange_stages(sizes):
    group, dom = sizes
    dom_bits = [1 << i for i in range(dom.bit_length() - 1)]
    group_bits = [dom << i for i in range(group.bit_length() - 1)]
    bits = dom_bits[1:2] + group_bits + dom_bits[2:]
    stages = [dom_bits[:1]]
    while bits:
        pair, bits = bits[:2], bits[2:]
        stages.append([pair[-1], pair[0], sum(pair)] if len(pair) == 2 else pair)
    return stages[:1] + [[bit | 1 for bit in stage] for stage in stages[1:]]


def sum_parts(values):
    sizes = [lax.axis_size(axis) for axis in AXES]
    devices = sizes[0] * sizes[1]
    if any(size & (size - 1) for size in sizes):
        return [lax.psum(values, AXES)]
    parts = [values]
    for stage in exchange_stages(sizes):
        total = functools.reduce(jnp.add, parts)
        parts = [total]
        for bit in stage:
            pairs = [(i, i ^ bit) for i in range(devices)]
            parts.append(lax.ppermute(total, AXES, pairs))
    return parts


def body(prior_basis, section_state, source, diag_blocks, coupling, neighbour_index, slot_count):
    blocks, block, columns = prior_basis.shape
    packed = pack(prior_basis, section_state)
    outer, inner = halo(packed, prior_basis, section_state)
    partial, base, near_coupling, near_index, near_count = pl.pallas_call(
        local_kernel,
        out_shape=(
            pltpu.VMEM(prior_basis.shape, F32),
            pltpu.VMEM(source.shape, F32),
            pltpu.VMEM(coupling.shape, BF16),
            pltpu.SMEM(neighbour_index.shape, jnp.int32),
            pltpu.SMEM(slot_count.shape, jnp.int32),
        ),
        in_specs=[smem()] * 2 + [vmem()] * 3 + [pl.BlockSpec(memory_space=pl.ANY)],
        out_specs=(vmem(),) * 3 + (smem(),) * 2,
        scratch_shapes=[pltpu.SemaphoreType.DMA],
        compiler_params=pltpu.CompilerParams(vmem_limit_bytes=VMEM_LIMIT),
        name="local_part",
    )(*far(neighbour_index, slot_count), *near(packed), *far(source, diag_blocks, coupling))
    _, rhs, image, sums = pl.pallas_call(
        shared_kernel,
        out_shape=(
            pltpu.VMEM(prior_basis.shape, F32),
            pltpu.VMEM(source.shape, F32),
            pltpu.VMEM(prior_basis.shape, BF16),
            pltpu.VMEM((block // 2 + 8, columns), F32),
        ),
        in_specs=[smem()] * 2 + [vmem()] * 5,
        out_specs=(vmem(),) * 4,
        input_output_aliases={5: 0, 6: 1},
        compiler_params=pltpu.CompilerParams(vmem_limit_bytes=VMEM_LIMIT),
        name="shared_part",
    )(
        *(pltpu.with_memory_space_constraint(array, pltpu.SMEM) for array in (near_index, near_count)),
        *near(inner, outer, near_coupling, partial, base),
    )
    parts = sum_parts(sums)
    rows_total = blocks * block * lax.axis_size("group") * lax.axis_size("dom")
    return pl.pallas_call(
        functools.partial(finish_kernel, rows_total=float(rows_total)),
        out_shape=(
            jax.ShapeDtypeStruct(prior_basis.shape, BF16),
            jax.ShapeDtypeStruct(prior_basis.shape, BF16),
            jax.ShapeDtypeStruct(source.shape, F32),
            jax.ShapeDtypeStruct(source.shape, F32),
        ),
        in_specs=[vmem()] * (len(parts) + 3),
        out_specs=(vmem(),) * 4,
        scratch_shapes=[pltpu.VMEM((block, columns), F32)] * 2,
        compiler_params=pltpu.CompilerParams(vmem_limit_bytes=VMEM_LIMIT),
        name="finish",
    )(*near(*parts, image, packed, rhs))


def solution(mesh):
    rows = P(AXES, None)
    cubes = P(AXES, None, None)
    return jax.shard_map(
        body,
        mesh=mesh,
        in_specs=(cubes, rows, rows, cubes, P(AXES, None, None, None), rows, P(AXES)),
        out_specs=(cubes, cubes, rows, rows),
        check_vma=False,
    )
```

```python
import functools

import jax
import jax.numpy as jnp
from jax import lax
from jax.experimental import pallas as pl
from jax.experimental.pallas import tpu as pltpu
from jax.sharding import PartitionSpec as P

HALO = 4
PANEL = 8
VMEM_LIMIT = 16 << 20
section_step = 0.25
AXES = ("group", "dom")
F32 = jnp.float32
BF16 = jnp.bfloat16

NN = (((1,), (0,)), ((), ()))
NT = (((1,), (1,)), ((), ()))
TN = (((0,), (0,)), ((), ()))


def dot(a, b, dims):
    return lax.dot_general(a, b, dims, preferred_element_type=F32)


def split_rows(row, count):
    sub = lax.broadcasted_iota(jnp.int32, (16, row.shape[1]), 0)
    rows = jnp.zeros((16, row.shape[1]), F32)
    rest = row
    for part in range(count):
        piece = rest.astype(BF16).astype(F32)
        rows = jnp.where(sub == part, piece, rows)
        rest = rest - piece
    return rows.astype(BF16)


def stack_rows(rows):
    return jnp.concatenate([jnp.broadcast_to(row, (16, row.shape[1])) for row in rows], axis=1).astype(BF16)


def pack_kernel(basis_ref, state_ref, packed_ref, rows_ref, sems):
    rows = basis_ref.shape[0]
    copy = pltpu.make_async_copy(basis_ref, packed_ref.at[pl.ds(0, rows)], sems.at[0])
    copy.start()
    state_copy = pltpu.make_async_copy(state_ref, rows_ref, sems.at[1])
    state_copy.start()
    state_copy.wait()
    state = rows_ref[...].astype(F32)
    spare = jnp.zeros((packed_ref.shape[0] - rows - state.shape[0], state.shape[1]), F32)
    packed_ref[rows:] = jnp.concatenate([state, spare], axis=0).astype(BF16)
    copy.wait()


def state_of(packed_ref, rows, count):
    return packed_ref[rows:].astype(F32)[:count]


def block_of(packed_ref, pick, block):
    return packed_ref[pl.ds(pl.multiple_of(pick * block, block), block)]


def local_kernel(
    index_ref,
    count_ref,
    packed_ref,
    source_ref,
    diag_ref,
    coupling_ref,
    partial_ref,
    base_ref,
    near_coupling_ref,
    near_index_ref,
    near_count_ref,
    sem,
):
    copy = pltpu.make_async_copy(coupling_ref, near_coupling_ref, sem)
    copy.start()
    blocks, block, _ = diag_ref.shape
    slots = coupling_ref.shape[1]
    for b in range(blocks):
        near_count_ref[b] = count_ref[b]
        for s in range(slots):
            near_index_ref[b, s] = index_ref[b, s]
    state = state_of(packed_ref, blocks * block, blocks)
    state_rows = [state[b : b + 1] for b in range(blocks)]
    copy.wait()
    for b in range(blocks):
        left, right, rows = [diag_ref[b]], [block_of(packed_ref, b, block)], [state_rows[b]]
        for s in range(2, slots):
            pick = index_ref[b, s] - HALO
            live = (count_ref[b] > s) & (pick >= 0) & (pick < blocks)
            pick = jnp.clip(pick, 0, blocks - 1)
            left.append(near_coupling_ref[b, s])
            right.append(jnp.where(live, block_of(packed_ref, pick, block), jnp.zeros((block, block), BF16)))
            row = state_rows[0]
            for i in range(1, blocks):
                row = jnp.where(pick == i, state_rows[i], row)
            rows.append(jnp.where(live, row, 0.0))
        left = jnp.concatenate(left, axis=1)
        partial_ref[b] = dot(left, jnp.concatenate(right, axis=0), NN)
        state_image = dot(stack_rows(rows), left, NT)[:1]
        base_ref[b : b + 1, :] = state_rows[b] + section_step * (source_ref[b : b + 1, :] - state_image)


def shared_kernel(
    index_ref,
    count_ref,
    inner_ref,
    outer_ref,
    coupling_ref,
    _partial_in_ref,
    _base_in_ref,
    partial_ref,
    rhs_ref,
    image_ref,
    sums_ref,
):
    blocks, block, _ = image_ref.shape
    here = lax.axis_index("dom")
    odd = here % 2 == 1
    first, last = here == 0, here == lax.axis_size("dom") - 1
    inner_state = state_of(inner_ref, HALO * block, HALO)
    outer_state = state_of(outer_ref, HALO * block, HALO)
    lower_state = jnp.where(first, 0.0, jnp.where(odd, inner_state, outer_state))
    upper_state = jnp.where(last, 0.0, jnp.where(odd, outer_state, inner_state))
    nothing = jnp.zeros((block, block), BF16)

    def lower(pick):
        picked = jnp.where(odd, block_of(inner_ref, pick, block), block_of(outer_ref, pick, block))
        return jnp.where(first, nothing, picked)

    def upper(pick):
        picked = jnp.where(odd, block_of(outer_ref, pick, block), block_of(inner_ref, pick, block))
        return jnp.where(last, nothing, picked)

    def chosen(rows, pick):
        row = rows[:1]
        for i in range(1, HALO):
            row = jnp.where(pick == i, rows[i : i + 1], row)
        return row

    for b in range(blocks):
        for s in range(2, coupling_ref.shape[1]):
            pick = index_ref[b, s]
            above = pick - HALO - blocks

            @pl.when((count_ref[b] > s) & ((pick < HALO) | (above >= 0)))
            def _(b=b, s=s, pick=pick, above=above):
                at = jnp.where(above >= 0, above, pick)
                picked = jnp.where(above >= 0, upper(at), lower(at))
                row = jnp.where(above >= 0, chosen(upper_state, at), chosen(lower_state, at))
                left = coupling_ref[b, s]
                partial_ref[b] += dot(left, picked, NN)
                rhs_ref[b : b + 1, :] -= section_step * dot(stack_rows([row]), left, NT)[:1]

    gram = jnp.zeros((block, block), F32)
    moment = jnp.zeros((16, block), F32)
    for b in range(blocks):
        below, above = index_ref[b, 0], index_ref[b, 1] - HALO - blocks
        left = jnp.concatenate([coupling_ref[b, 0], coupling_ref[b, 1]], axis=1)
        right = jnp.concatenate([lower(below), upper(above)], axis=0)
        image = (partial_ref[b] + dot(left, right, NN)).astype(BF16)
        rows = stack_rows([chosen(lower_state, below), chosen(upper_state, above)])
        rhs = rhs_ref[b : b + 1, :] - section_step * dot(rows, left, NT)[:1]
        image_ref[b] = image
        rhs_ref[b : b + 1, :] = rhs
        gram = gram + dot(image, image, TN)
        moment = moment + dot(split_rows(rhs, 3), image, NN)
    half = block // 2
    top, bottom = gram[:half], gram[half:]
    sub = lax.broadcasted_iota(jnp.int32, (half, block), 0)
    lane = lax.broadcasted_iota(jnp.int32, (half, block), 1)
    sums_ref[:half] = jnp.where(lane < sub, pltpu.roll(bottom, half, 1), top)
    pivots = jnp.sum(jnp.where(lane == sub + half, bottom, 0.0), axis=0, keepdims=True)
    row = lax.broadcasted_iota(jnp.int32, (8, block), 0)
    total = jnp.sum(moment, axis=0, keepdims=True)
    sums_ref[half:] = jnp.where(row == 0, pivots, jnp.where(row == 1, total, 0.0))


def spread(value, shape):
    return jnp.broadcast_to(value, shape)


def eliminate(rows, wide_ref, pair_ref):
    order = rows[0].shape[1]
    panels = len(rows)
    rows = list(rows)
    shape = (PANEL, order)
    lane = lax.broadcasted_iota(jnp.int32, shape, 1)
    sub = lax.broadcasted_iota(jnp.int32, shape, 0)

    def update(q, c, solved):
        terms = [spread(rows[q][:, c + k : c + k + 1], shape) * solved[k] for k in range(PANEL)]
        while len(terms) > 1:
            terms = [x + y for x, y in zip(terms[::2], terms[1::2])]
        rows[q] = jnp.where((lane >= c) & (lane < c + PANEL), 0.0, rows[q]) - terms[0]

    done = []
    waiting = []
    for p in range(panels):
        c = p * PANEL
        panel = (lane >= c) & (lane < c + PANEL)
        columns = [spread(rows[p][:, c + j : c + j + 1], shape) for j in range(PANEL)]
        at = p % 2 * PANEL
        wide_ref[at : at + PANEL, :] = jnp.where(panel, 0.0, rows[p])
        for j in range(PANEL):
            base = (at + j) * PANEL
            pair_ref[base : base + PANEL, :] = columns[j]
        wide = [spread(wide_ref[at + i : at + i + 1, :], shape) for i in range(PANEL)]
        a = [
            [
                spread(pair_ref[(at + j) * PANEL + i : (at + j) * PANEL + i + 1, :], shape) if j >= i else None
                for j in range(PANEL)
            ]
            for i in range(PANEL)
        ]
        out = jnp.zeros(shape, F32)
        solved = [None] * PANEL
        for k in range(PANEL):
            pivot = a[k][k]
            root = lax.rsqrt(pivot)
            if k % 2 == 0:
                inv = pl.reciprocal(pivot, approx=True)
                minor = pivot * a[k + 1][k + 1] - a[k][k + 1] * a[k][k + 1]
                next_inv = pivot * pl.reciprocal(minor, approx=True)
            else:
                inv = next_inv
            unit = jnp.where(lane == c + k, 1.0, wide[k])
            out = jnp.where(sub == k, unit * root, out)
            solved[k] = unit * inv
            factor = [None] * PANEL
            for j in range(k + 1, PANEL):
                factor[j] = a[k][j] * inv
            for i in range(k + 1, PANEL):
                for j in range(i, PANEL):
                    a[i][j] = a[i][j] - factor[i] * a[k][j]
                wide[i] = wide[i] - factor[i] * unit
            for i in range(k):
                for j in range(k + 1, PANEL):
                    a[i][j] = a[i][j] - a[i][k] * factor[j]
                solved[i] = solved[i] - a[i][k] * solved[k]
            for j in range(k + 1, PANEL):
                a[k][j] = factor[j]
            share = pl.cdiv(len(waiting), PANEL - k)
            for job in waiting[:share]:
                update(*job)
            waiting = waiting[share:]
        if p + 1 < panels:
            update(p + 1, c, solved)
        waiting = [(q, c, solved) for q in range(p + 2, panels)]
        done.append(jnp.where(lane <= c + sub, out, 0.0))
    return done


def finish_kernel(*refs, rows_total):
    sum_refs = refs[:-11]
    image_ref, packed_ref, rhs_ref, new_ref, new_image_ref, guess_ref, residual_ref = refs[-11:-4]
    gram_ref, factor_ref, wide_ref, pair_ref = refs[-4:]
    blocks, block, _ = image_ref.shape
    half = block // 2
    packed = sum_refs[0][...]
    for ref in sum_refs[1:]:
        packed = packed + ref[...]
    packed = packed * (1.0 / rows_total)
    top = packed[:half]
    sub = lax.broadcasted_iota(jnp.int32, (half, block), 0)
    lane = lax.broadcasted_iota(jnp.int32, (half, block), 1)
    upper = jnp.where(lane >= sub, top, 0.0)
    shifted = pltpu.roll(top, half, 1)
    lower = jnp.where((lane >= half) & (lane < sub + half), shifted, 0.0)
    pivots = packed[half : half + 1]
    lower = jnp.where(lane == sub + half, pivots, lower)
    once = jnp.concatenate([upper, lower], axis=0)
    row = lax.broadcasted_iota(jnp.int32, (block, block), 0)
    col = lax.broadcasted_iota(jnp.int32, (block, block), 1)
    gram_ref[...] = once + jnp.where(row == col, 0.0, once.T)
    done = eliminate([gram_ref[p : p + PANEL, :] for p in range(0, block, PANEL)], wide_ref, pair_ref)
    for p, panel in enumerate(done):
        factor_ref[p * PANEL : (p + 1) * PANEL, :] = panel
    factor = factor_ref[...]
    moment = packed[half + 1 : half + 2]
    coefficients = jnp.sum(factor * moment, axis=1, keepdims=True)
    weights = jnp.sum(factor * coefficients, axis=0, keepdims=True)
    weights = split_rows(weights, 3)
    high = factor.astype(BF16)
    low = (factor - high.astype(F32)).astype(BF16)
    both = jnp.concatenate([high, low], axis=1)
    for b in range(blocks):
        image, basis = image_ref[b], block_of(packed_ref, b, block)
        new_image_ref[b] = dot(jnp.concatenate([image, image], axis=1), both, NT).astype(BF16)
        new_ref[b] = dot(jnp.concatenate([basis, basis], axis=1), both, NT).astype(BF16)
        guess = jnp.sum(dot(weights, basis, NT), axis=0, keepdims=True)
        guess_ref[b : b + 1, :] = guess
        fitted = jnp.sum(dot(weights, image, NT), axis=0, keepdims=True)
        residual_ref[b : b + 1, :] = rhs_ref[b : b + 1, :] - fitted


def near(*arrays):
    return [pltpu.with_memory_space_constraint(array, pltpu.VMEM) for array in arrays]


def far(*arrays):
    return [pltpu.with_memory_space_constraint(array, pltpu.HBM) for array in arrays]


def vmem():
    return pl.BlockSpec(memory_space=pltpu.VMEM)


def smem():
    return pl.BlockSpec(memory_space=pltpu.SMEM)


def pack(basis, state):
    blocks, block, columns = basis.shape
    rows = blocks * block
    return pl.pallas_call(
        pack_kernel,
        out_shape=pltpu.VMEM((rows + 16 * pl.cdiv(blocks, 16), columns), BF16),
        in_specs=[pl.BlockSpec(memory_space=pl.ANY)] * 2,
        out_specs=vmem(),
        scratch_shapes=[pltpu.VMEM(state.shape, BF16), pltpu.SemaphoreType.DMA((2,))],
        compiler_params=pltpu.CompilerParams(vmem_limit_bytes=VMEM_LIMIT),
        name="pack",
    )(*far(basis.reshape(rows, columns), state))


def swap_pairs(parity, groups, devices):
    pairs = []
    for group in range(groups):
        for device in range(devices):
            other = device + 1 if device % 2 == parity else device - 1
            if 0 <= other < devices:
                pairs.append((group * devices + device, group * devices + other))
            else:
                twin = group ^ 1 if group ^ 1 < groups else group
                pairs.append((group * devices + device, twin * devices + device))
    return pairs


def halo(packed, basis, state):
    groups, devices = (lax.axis_size(axis) for axis in AXES)
    odd = lax.axis_index("dom") % 2
    got = []
    for parity in (1, 0):
        sent = packed
        if basis.shape[0] > HALO:
            up = odd == parity
            sent = pack(*(jnp.where(up, whole[-HALO:], whole[:HALO]) for whole in (basis, state)))
        got.append(lax.ppermute(sent, AXES, swap_pairs(parity, groups, devices)))
    return got


def exchange_stages(sizes):
    group, dom = sizes
    dom_bits = [1 << i for i in range(dom.bit_length() - 1)]
    group_bits = [dom << i for i in range(group.bit_length() - 1)]
    bits = dom_bits[1:2] + group_bits + dom_bits[2:]
    stages = [dom_bits[:1]]
    while bits:
        pair, bits = bits[:2], bits[2:]
        stages.append([pair[-1], pair[0], sum(pair)] if len(pair) == 2 else pair)
    return stages[:1] + [[bit | 1 for bit in stage] for stage in stages[1:]]


def sum_parts(values):
    sizes = [lax.axis_size(axis) for axis in AXES]
    devices = sizes[0] * sizes[1]
    if any(size & (size - 1) for size in sizes):
        return [lax.psum(values, AXES)]
    parts = [values]
    for stage in exchange_stages(sizes):
        total = functools.reduce(jnp.add, parts)
        parts = [total]
        for bit in stage:
            pairs = [(i, i ^ bit) for i in range(devices)]
            parts.append(lax.ppermute(total, AXES, pairs))
    return parts


def finish(parts, image, packed, rhs, rows_total):
    blocks, block, columns = image.shape
    return pl.pallas_call(
        functools.partial(finish_kernel, rows_total=rows_total),
        out_shape=(
            jax.ShapeDtypeStruct(image.shape, BF16),
            jax.ShapeDtypeStruct(image.shape, BF16),
            jax.ShapeDtypeStruct(rhs.shape, F32),
            jax.ShapeDtypeStruct(rhs.shape, F32),
        ),
        in_specs=[vmem()] * (len(parts) + 3),
        out_specs=(vmem(),) * 4,
        scratch_shapes=[pltpu.VMEM((block, columns), F32)] * 2 + [pltpu.VMEM((2 * PANEL, columns), F32), pltpu.VMEM((2 * PANEL * PANEL, columns), F32)],
        compiler_params=pltpu.CompilerParams(vmem_limit_bytes=VMEM_LIMIT),
        name="finish",
    )(*near(*parts, image, packed, rhs))


def body(prior_basis, section_state, source, diag_blocks, coupling, neighbour_index, slot_count):
    blocks, block, columns = prior_basis.shape
    packed = pack(prior_basis, section_state)
    outer, inner = halo(packed, prior_basis, section_state)
    partial, base, near_coupling, near_index, near_count = pl.pallas_call(
        local_kernel,
        out_shape=(
            pltpu.VMEM(prior_basis.shape, F32),
            pltpu.VMEM(source.shape, F32),
            pltpu.VMEM(coupling.shape, BF16),
            pltpu.SMEM(neighbour_index.shape, jnp.int32),
            pltpu.SMEM(slot_count.shape, jnp.int32),
        ),
        in_specs=[smem()] * 2 + [vmem()] * 3 + [pl.BlockSpec(memory_space=pl.ANY)],
        out_specs=(vmem(),) * 3 + (smem(),) * 2,
        scratch_shapes=[pltpu.SemaphoreType.DMA],
        compiler_params=pltpu.CompilerParams(vmem_limit_bytes=VMEM_LIMIT),
        name="local_part",
    )(*far(neighbour_index, slot_count), *near(packed), *far(source, diag_blocks, coupling))
    _, rhs, image, sums = pl.pallas_call(
        shared_kernel,
        out_shape=(
            pltpu.VMEM(prior_basis.shape, F32),
            pltpu.VMEM(source.shape, F32),
            pltpu.VMEM(prior_basis.shape, BF16),
            pltpu.VMEM((block // 2 + 8, columns), F32),
        ),
        in_specs=[smem()] * 2 + [vmem()] * 5,
        out_specs=(vmem(),) * 4,
        input_output_aliases={5: 0, 6: 1},
        compiler_params=pltpu.CompilerParams(vmem_limit_bytes=VMEM_LIMIT),
        name="shared_part",
    )(
        *(pltpu.with_memory_space_constraint(array, pltpu.SMEM) for array in (near_index, near_count)),
        *near(inner, outer, near_coupling, partial, base),
    )
    parts = sum_parts(sums)
    rows_total = blocks * block * lax.axis_size("group") * lax.axis_size("dom")
    return finish(parts, image, packed, rhs, float(rows_total))


def solution(mesh):
    rows = P(AXES, None)
    cubes = P(AXES, None, None)
    return jax.shard_map(
        body,
        mesh=mesh,
        in_specs=(cubes, rows, rows, cubes, P(AXES, None, None, None), rows, P(AXES)),
        out_specs=(cubes, cubes, rows, rows),
        check_vma=False,
    )
```

```python
import functools

import jax
import jax.numpy as jnp
from jax import lax
from jax.experimental import pallas as pl
from jax.experimental.pallas import tpu as pltpu
from jax.sharding import PartitionSpec as P

HALO = 4
PANEL = 8
VMEM_LIMIT = 16 << 20
section_step = 0.25
AXES = ("group", "dom")
F32 = jnp.float32
BF16 = jnp.bfloat16

NN = (((1,), (0,)), ((), ()))
NT = (((1,), (1,)), ((), ()))
TN = (((0,), (0,)), ((), ()))


def dot(a, b, dims):
    return lax.dot_general(a, b, dims, preferred_element_type=F32)


def split_rows(row, count):
    sub = lax.broadcasted_iota(jnp.int32, (16, row.shape[1]), 0)
    rows = jnp.zeros((16, row.shape[1]), F32)
    rest = row
    for part in range(count):
        piece = rest.astype(BF16).astype(F32)
        rows = jnp.where(sub == part, piece, rows)
        rest = rest - piece
    return rows.astype(BF16)


def stack_rows(rows):
    return jnp.concatenate([jnp.broadcast_to(row, (16, row.shape[1])) for row in rows], axis=1).astype(BF16)


def pack_kernel(basis_ref, state_ref, packed_ref, rows_ref, sems):
    rows = basis_ref.shape[0]
    copy = pltpu.make_async_copy(basis_ref, packed_ref.at[pl.ds(0, rows)], sems.at[0])
    copy.start()
    state_copy = pltpu.make_async_copy(state_ref, rows_ref, sems.at[1])
    state_copy.start()
    state_copy.wait()
    state = rows_ref[...].astype(F32)
    spare = jnp.zeros((packed_ref.shape[0] - rows - state.shape[0], state.shape[1]), F32)
    packed_ref[rows:] = jnp.concatenate([state, spare], axis=0).astype(BF16)
    copy.wait()


def state_of(packed_ref, rows, count):
    return packed_ref[rows:].astype(F32)[:count]


def block_of(packed_ref, pick, block):
    return packed_ref[pl.ds(pl.multiple_of(pick * block, block), block)]


def local_kernel(
    index_ref,
    count_ref,
    packed_ref,
    source_ref,
    diag_ref,
    coupling_ref,
    partial_ref,
    base_ref,
    near_coupling_ref,
    near_index_ref,
    near_count_ref,
    sem,
):
    copy = pltpu.make_async_copy(coupling_ref, near_coupling_ref, sem)
    copy.start()
    blocks, block, _ = diag_ref.shape
    slots = coupling_ref.shape[1]
    for b in range(blocks):
        near_count_ref[b] = count_ref[b]
        for s in range(slots):
            near_index_ref[b, s] = index_ref[b, s]
    state = state_of(packed_ref, blocks * block, blocks)
    state_rows = [state[b : b + 1] for b in range(blocks)]
    copy.wait()
    for b in range(blocks):
        left, right, rows = [diag_ref[b]], [block_of(packed_ref, b, block)], [state_rows[b]]
        for s in range(2, slots):
            pick = index_ref[b, s] - HALO
            live = (count_ref[b] > s) & (pick >= 0) & (pick < blocks)
            pick = jnp.clip(pick, 0, blocks - 1)
            left.append(near_coupling_ref[b, s])
            right.append(jnp.where(live, block_of(packed_ref, pick, block), jnp.zeros((block, block), BF16)))
            row = state_rows[0]
            for i in range(1, blocks):
                row = jnp.where(pick == i, state_rows[i], row)
            rows.append(jnp.where(live, row, 0.0))
        left = jnp.concatenate(left, axis=1)
        partial_ref[b] = dot(left, jnp.concatenate(right, axis=0), NN)
        state_image = dot(stack_rows(rows), left, NT)[:1]
        base_ref[b : b + 1, :] = state_rows[b] + section_step * (source_ref[b : b + 1, :] - state_image)


def shared_kernel(
    index_ref,
    count_ref,
    inner_ref,
    outer_ref,
    coupling_ref,
    _partial_in_ref,
    _base_in_ref,
    partial_ref,
    rhs_ref,
    image_ref,
    sums_ref,
):
    blocks, block, _ = image_ref.shape
    here = lax.axis_index("dom")
    odd = here % 2 == 1
    first, last = here == 0, here == lax.axis_size("dom") - 1
    inner_state = state_of(inner_ref, HALO * block, HALO)
    outer_state = state_of(outer_ref, HALO * block, HALO)
    lower_state = jnp.where(first, 0.0, jnp.where(odd, inner_state, outer_state))
    upper_state = jnp.where(last, 0.0, jnp.where(odd, outer_state, inner_state))
    nothing = jnp.zeros((block, block), BF16)

    def lower(pick):
        picked = jnp.where(odd, block_of(inner_ref, pick, block), block_of(outer_ref, pick, block))
        return jnp.where(first, nothing, picked)

    def upper(pick):
        picked = jnp.where(odd, block_of(outer_ref, pick, block), block_of(inner_ref, pick, block))
        return jnp.where(last, nothing, picked)

    def chosen(rows, pick):
        row = rows[:1]
        for i in range(1, HALO):
            row = jnp.where(pick == i, rows[i : i + 1], row)
        return row

    for b in range(blocks):
        for s in range(2, coupling_ref.shape[1]):
            pick = index_ref[b, s]
            above = pick - HALO - blocks

            @pl.when((count_ref[b] > s) & ((pick < HALO) | (above >= 0)))
            def _(b=b, s=s, pick=pick, above=above):
                at = jnp.where(above >= 0, above, pick)
                picked = jnp.where(above >= 0, upper(at), lower(at))
                row = jnp.where(above >= 0, chosen(upper_state, at), chosen(lower_state, at))
                left = coupling_ref[b, s]
                partial_ref[b] += dot(left, picked, NN)
                rhs_ref[b : b + 1, :] -= section_step * dot(stack_rows([row]), left, NT)[:1]

    gram = jnp.zeros((block, block), F32)
    moment = jnp.zeros((16, block), F32)
    for b in range(blocks):
        below, above = index_ref[b, 0], index_ref[b, 1] - HALO - blocks
        left = jnp.concatenate([coupling_ref[b, 0], coupling_ref[b, 1]], axis=1)
        right = jnp.concatenate([lower(below), upper(above)], axis=0)
        image = (partial_ref[b] + dot(left, right, NN)).astype(BF16)
        rows = stack_rows([chosen(lower_state, below), chosen(upper_state, above)])
        rhs = rhs_ref[b : b + 1, :] - section_step * dot(rows, left, NT)[:1]
        image_ref[b] = image
        rhs_ref[b : b + 1, :] = rhs
        gram = gram + dot(image, image, TN)
        moment = moment + dot(split_rows(rhs, 3), image, NN)
    half = block // 2
    top, bottom = gram[:half], gram[half:]
    sub = lax.broadcasted_iota(jnp.int32, (half, block), 0)
    lane = lax.broadcasted_iota(jnp.int32, (half, block), 1)
    sums_ref[:half] = jnp.where(lane < sub, pltpu.roll(bottom, half, 1), top)
    pivots = jnp.where(lane == sub, top, jnp.where(lane == sub + half, bottom, 0.0))
    pivots = jnp.sum(pivots, axis=0, keepdims=True)
    row = lax.broadcasted_iota(jnp.int32, (8, block), 0)
    total = jnp.sum(moment, axis=0, keepdims=True)
    sums_ref[half:] = jnp.where(row == 0, pivots, jnp.where(row == 1, total, 0.0))


def spread(value, shape):
    return jnp.broadcast_to(value, shape)


def eliminate(rows, wide_ref, pair_ref):
    order = rows[0].shape[1]
    panels = len(rows)
    rows = list(rows)
    shape = (PANEL, order)
    lane = lax.broadcasted_iota(jnp.int32, shape, 1)
    sub = lax.broadcasted_iota(jnp.int32, shape, 0)

    def update(q, c, solved):
        terms = [spread(rows[q][:, c + k : c + k + 1], shape) * solved[k] for k in range(PANEL)]
        while len(terms) > 1:
            terms = [x + y for x, y in zip(terms[::2], terms[1::2])]
        rows[q] = jnp.where((lane >= c) & (lane < c + PANEL), 0.0, rows[q]) - terms[0]

    done = []
    waiting = []
    for p in range(panels):
        c = p * PANEL
        panel = (lane >= c) & (lane < c + PANEL)
        columns = [spread(rows[p][:, c + j : c + j + 1], shape) for j in range(PANEL)]
        at = p % 2 * PANEL
        wide_ref[at : at + PANEL, :] = jnp.where(panel, 0.0, rows[p])
        for j in range(PANEL):
            base = (at + j) * PANEL
            pair_ref[base : base + PANEL, :] = columns[j]
        wide = [spread(wide_ref[at + i : at + i + 1, :], shape) for i in range(PANEL)]
        a = [
            [
                spread(pair_ref[(at + j) * PANEL + i : (at + j) * PANEL + i + 1, :], shape) if j >= i else None
                for j in range(PANEL)
            ]
            for i in range(PANEL)
        ]
        out = jnp.zeros(shape, F32)
        solved = [None] * PANEL
        for k in range(PANEL):
            pivot = a[k][k]
            root = lax.rsqrt(pivot)
            if k % 2 == 0:
                inv = pl.reciprocal(pivot, approx=True)
                minor = pivot * a[k + 1][k + 1] - a[k][k + 1] * a[k][k + 1]
                next_inv = pivot * pl.reciprocal(minor, approx=True)
            else:
                inv = next_inv
            unit = jnp.where(lane == c + k, 1.0, wide[k])
            out = jnp.where(sub == k, unit * root, out)
            solved[k] = unit * inv
            factor = [None] * PANEL
            for j in range(k + 1, PANEL):
                factor[j] = a[k][j] * inv
            for i in range(k + 1, PANEL):
                for j in range(i, PANEL):
                    a[i][j] = a[i][j] - factor[i] * a[k][j]
                wide[i] = wide[i] - factor[i] * unit
            for i in range(k):
                for j in range(k + 1, PANEL):
                    a[i][j] = a[i][j] - a[i][k] * factor[j]
                solved[i] = solved[i] - a[i][k] * solved[k]
            for j in range(k + 1, PANEL):
                a[k][j] = factor[j]
            share = pl.cdiv(len(waiting), PANEL - k)
            for job in waiting[:share]:
                update(*job)
            waiting = waiting[share:]
        if p + 1 < panels:
            update(p + 1, c, solved)
        waiting = [(q, c, solved) for q in range(p + 2, panels)]
        done.append(jnp.where(lane <= c + sub, out, 0.0))
    return done


def finish_kernel(*refs, rows_total):
    sum_refs = refs[:-11]
    image_ref, packed_ref, rhs_ref, new_ref, new_image_ref, guess_ref, residual_ref = refs[-11:-4]
    gram_ref, factor_ref, wide_ref, pair_ref = refs[-4:]
    blocks, block, _ = image_ref.shape
    half = block // 2
    packed = sum_refs[0][...]
    for ref in sum_refs[1:]:
        packed = packed + ref[...]
    top, pivots = packed[:half], packed[half : half + 1]
    sub = lax.broadcasted_iota(jnp.int32, (half, block), 0)
    lane = lax.broadcasted_iota(jnp.int32, (half, block), 1)
    upper = jnp.where(lane >= sub, top, 0.0)
    lower = jnp.where((lane >= half) & (lane < sub + half), pltpu.roll(top, half, 1), 0.0)
    lower = jnp.where(lane == sub + half, pivots, lower)
    once = jnp.concatenate([upper, lower], axis=0)
    row = lax.broadcasted_iota(jnp.int32, (block, block), 0)
    col = lax.broadcasted_iota(jnp.int32, (block, block), 1)
    across = lax.rsqrt(pivots)
    half_scaled = (once * across).T * across
    gram_ref[...] = half_scaled + jnp.where(row == col, 0.0, half_scaled.T)
    done = eliminate([gram_ref[p : p + PANEL, :] for p in range(0, block, PANEL)], wide_ref, pair_ref)
    for p, panel in enumerate(done):
        factor_ref[p * PANEL : (p + 1) * PANEL, :] = panel
    factor = factor_ref[...] * (across * rows_total**0.5)
    moment = packed[half + 1 : half + 2] * (1.0 / rows_total)
    coefficients = jnp.sum(factor * moment, axis=1, keepdims=True)
    weights = jnp.sum(factor * coefficients, axis=0, keepdims=True)
    weights = split_rows(weights, 3)
    high = factor.astype(BF16)
    low = (factor - high.astype(F32)).astype(BF16)
    both = jnp.concatenate([high, low], axis=1)
    for b in range(blocks):
        image, basis = image_ref[b], block_of(packed_ref, b, block)
        new_image_ref[b] = dot(jnp.concatenate([image, image], axis=1), both, NT).astype(BF16)
        new_ref[b] = dot(jnp.concatenate([basis, basis], axis=1), both, NT).astype(BF16)
        guess = jnp.sum(dot(weights, basis, NT), axis=0, keepdims=True)
        guess_ref[b : b + 1, :] = guess
        fitted = jnp.sum(dot(weights, image, NT), axis=0, keepdims=True)
        residual_ref[b : b + 1, :] = rhs_ref[b : b + 1, :] - fitted


def near(*arrays):
    return [pltpu.with_memory_space_constraint(array, pltpu.VMEM) for array in arrays]


def far(*arrays):
    return [pltpu.with_memory_space_constraint(array, pltpu.HBM) for array in arrays]


def vmem():
    return pl.BlockSpec(memory_space=pltpu.VMEM)


def smem():
    return pl.BlockSpec(memory_space=pltpu.SMEM)


def pack(basis, state):
    blocks, block, columns = basis.shape
    rows = blocks * block
    return pl.pallas_call(
        pack_kernel,
        out_shape=pltpu.VMEM((rows + 16 * pl.cdiv(blocks, 16), columns), BF16),
        in_specs=[pl.BlockSpec(memory_space=pl.ANY)] * 2,
        out_specs=vmem(),
        scratch_shapes=[pltpu.VMEM(state.shape, BF16), pltpu.SemaphoreType.DMA((2,))],
        compiler_params=pltpu.CompilerParams(vmem_limit_bytes=VMEM_LIMIT),
        name="pack",
    )(*far(basis.reshape(rows, columns), state))


def swap_pairs(parity, groups, devices):
    pairs = []
    for group in range(groups):
        for device in range(devices):
            other = device + 1 if device % 2 == parity else device - 1
            if 0 <= other < devices:
                pairs.append((group * devices + device, group * devices + other))
            else:
                twin = group ^ 1 if group ^ 1 < groups else group
                pairs.append((group * devices + device, twin * devices + device))
    return pairs


def halo(packed, basis, state):
    groups, devices = (lax.axis_size(axis) for axis in AXES)
    odd = lax.axis_index("dom") % 2
    got = []
    for parity in (1, 0):
        sent = packed
        if basis.shape[0] > HALO:
            up = odd == parity
            sent = pack(*(jnp.where(up, whole[-HALO:], whole[:HALO]) for whole in (basis, state)))
        got.append(lax.ppermute(sent, AXES, swap_pairs(parity, groups, devices)))
    return got


def exchange_stages(sizes):
    group, dom = sizes
    dom_bits = [1 << i for i in range(dom.bit_length() - 1)]
    group_bits = [dom << i for i in range(group.bit_length() - 1)]
    bits = group_bits[:1] + dom_bits[1:2] + dom_bits[2:] + group_bits[1:]
    stages = [dom_bits[:1], bits[:2] + [sum(bits[:2])], *([bit] for bit in bits[2:])]
    if len(dom_bits) < 2 or not group_bits:
        stages = [dom_bits[:1], *([bit] for bit in bits)]
    return stages[:1] + [[bit | 1 for bit in stage] for stage in stages[1:]]


def sum_parts(values):
    sizes = [lax.axis_size(axis) for axis in AXES]
    devices = sizes[0] * sizes[1]
    if any(size & (size - 1) for size in sizes):
        return [lax.psum(values, AXES)]
    parts = [values]
    for stage in exchange_stages(sizes):
        total = functools.reduce(jnp.add, parts)
        parts = [total]
        for bit in stage:
            pairs = [(i, i ^ bit) for i in range(devices)]
            parts.append(lax.ppermute(total, AXES, pairs))
    return parts


def finish(parts, image, packed, rhs, rows_total):
    blocks, block, columns = image.shape
    return pl.pallas_call(
        functools.partial(finish_kernel, rows_total=rows_total),
        out_shape=(
            jax.ShapeDtypeStruct(image.shape, BF16),
            jax.ShapeDtypeStruct(image.shape, BF16),
            jax.ShapeDtypeStruct(rhs.shape, F32),
            jax.ShapeDtypeStruct(rhs.shape, F32),
        ),
        in_specs=[vmem()] * (len(parts) + 3),
        out_specs=(vmem(),) * 4,
        scratch_shapes=[pltpu.VMEM((block, columns), F32)] * 2 + [pltpu.VMEM((2 * PANEL, columns), F32), pltpu.VMEM((2 * PANEL * PANEL, columns), F32)],
        compiler_params=pltpu.CompilerParams(vmem_limit_bytes=VMEM_LIMIT),
        name="finish",
    )(*near(*parts, image, packed, rhs))


def body(prior_basis, section_state, source, diag_blocks, coupling, neighbour_index, slot_count):
    blocks, block, columns = prior_basis.shape
    packed = pack(prior_basis, section_state)
    outer, inner = halo(packed, prior_basis, section_state)
    partial, base, near_coupling, near_index, near_count = pl.pallas_call(
        local_kernel,
        out_shape=(
            pltpu.VMEM(prior_basis.shape, F32),
            pltpu.VMEM(source.shape, F32),
            pltpu.VMEM(coupling.shape, BF16),
            pltpu.SMEM(neighbour_index.shape, jnp.int32),
            pltpu.SMEM(slot_count.shape, jnp.int32),
        ),
        in_specs=[smem()] * 2 + [vmem()] * 3 + [pl.BlockSpec(memory_space=pl.ANY)],
        out_specs=(vmem(),) * 3 + (smem(),) * 2,
        scratch_shapes=[pltpu.SemaphoreType.DMA],
        compiler_params=pltpu.CompilerParams(vmem_limit_bytes=VMEM_LIMIT),
        name="local_part",
    )(*far(neighbour_index, slot_count), *near(packed), *far(source, diag_blocks, coupling))
    _, rhs, image, sums = pl.pallas_call(
        shared_kernel,
        out_shape=(
            pltpu.VMEM(prior_basis.shape, F32),
            pltpu.VMEM(source.shape, F32),
            pltpu.VMEM(prior_basis.shape, BF16),
            pltpu.VMEM((block // 2 + 8, columns), F32),
        ),
        in_specs=[smem()] * 2 + [vmem()] * 5,
        out_specs=(vmem(),) * 4,
        input_output_aliases={5: 0, 6: 1},
        compiler_params=pltpu.CompilerParams(vmem_limit_bytes=VMEM_LIMIT),
        name="shared_part",
    )(
        *(pltpu.with_memory_space_constraint(array, pltpu.SMEM) for array in (near_index, near_count)),
        *near(inner, outer, near_coupling, partial, base),
    )
    parts = sum_parts(sums)
    rows_total = blocks * block * lax.axis_size("group") * lax.axis_size("dom")
    return finish(parts, image, packed, rhs, float(rows_total))


def solution(mesh):
    rows = P(AXES, None)
    cubes = P(AXES, None, None)
    return jax.shard_map(
        body,
        mesh=mesh,
        in_specs=(cubes, rows, rows, cubes, P(AXES, None, None, None), rows, P(AXES)),
        out_specs=(cubes, cubes, rows, rows),
        check_vma=False,
    )
```

```python
import functools

import jax
import jax.numpy as jnp
from jax import lax
from jax.experimental import pallas as pl
from jax.experimental.pallas import tpu as pltpu
from jax.sharding import PartitionSpec as P

HALO = 4
PANEL = 8
VMEM_LIMIT = 16 << 20
section_step = 0.25
AXES = ("group", "dom")
F32 = jnp.float32
BF16 = jnp.bfloat16

NN = (((1,), (0,)), ((), ()))
NT = (((1,), (1,)), ((), ()))
TN = (((0,), (0,)), ((), ()))


def dot(a, b, dims):
    return lax.dot_general(a, b, dims, preferred_element_type=F32)


def split_rows(row, count):
    sub = lax.broadcasted_iota(jnp.int32, (16, row.shape[1]), 0)
    rows = jnp.zeros((16, row.shape[1]), F32)
    rest = row
    for part in range(count):
        piece = rest.astype(BF16).astype(F32)
        rows = jnp.where(sub == part, piece, rows)
        rest = rest - piece
    return rows.astype(BF16)


def stack_rows(rows):
    return jnp.concatenate([jnp.broadcast_to(row, (16, row.shape[1])) for row in rows], axis=1).astype(BF16)


def pack_kernel(basis_ref, state_ref, packed_ref, rows_ref, sems):
    rows = basis_ref.shape[0]
    copy = pltpu.make_async_copy(basis_ref, packed_ref.at[pl.ds(0, rows)], sems.at[0])
    copy.start()
    state_copy = pltpu.make_async_copy(state_ref, rows_ref, sems.at[1])
    state_copy.start()
    state_copy.wait()
    state = rows_ref[...].astype(F32)
    spare = jnp.zeros((packed_ref.shape[0] - rows - state.shape[0], state.shape[1]), F32)
    packed_ref[rows:] = jnp.concatenate([state, spare], axis=0).astype(BF16)
    copy.wait()


def state_of(packed_ref, rows, count):
    return packed_ref[rows:].astype(F32)[:count]


def block_of(packed_ref, pick, block):
    return packed_ref[pl.ds(pl.multiple_of(pick * block, block), block)]


def local_kernel(
    index_ref,
    count_ref,
    packed_ref,
    source_ref,
    diag_ref,
    coupling_ref,
    partial_ref,
    base_ref,
    near_coupling_ref,
    near_index_ref,
    near_count_ref,
    facts_ref,
    sem,
):
    copy = pltpu.make_async_copy(coupling_ref, near_coupling_ref, sem)
    copy.start()
    blocks, block, _ = diag_ref.shape
    slots = coupling_ref.shape[1]
    here = lax.axis_index("dom")
    facts_ref[0] = here % 2
    facts_ref[1] = (here == 0).astype(jnp.int32)
    facts_ref[2] = (here == lax.axis_size("dom") - 1).astype(jnp.int32)
    shared = jnp.int32(0)
    for b in range(blocks):
        near_count_ref[b] = count_ref[b]
        for s in range(slots):
            near_index_ref[b, s] = index_ref[b, s]
        for s in range(2, slots):
            outside = (index_ref[b, s] < HALO) | (index_ref[b, s] >= HALO + blocks)
            shared += ((count_ref[b] > s) & outside).astype(jnp.int32)
    facts_ref[3] = shared
    state = state_of(packed_ref, blocks * block, blocks)
    state_rows = [state[b : b + 1] for b in range(blocks)]
    copy.wait()
    for b in range(blocks):
        left, right, rows = [diag_ref[b]], [block_of(packed_ref, b, block)], [state_rows[b]]
        for s in range(2, slots):
            pick = index_ref[b, s] - HALO
            live = (count_ref[b] > s) & (pick >= 0) & (pick < blocks)
            pick = jnp.clip(pick, 0, blocks - 1)
            left.append(near_coupling_ref[b, s])
            right.append(jnp.where(live, block_of(packed_ref, pick, block), jnp.zeros((block, block), BF16)))
            row = state_rows[0]
            for i in range(1, blocks):
                row = jnp.where(pick == i, state_rows[i], row)
            rows.append(jnp.where(live, row, 0.0))
        left = jnp.concatenate(left, axis=1)
        partial_ref[b] = dot(left, jnp.concatenate(right, axis=0), NN)
        state_image = dot(stack_rows(rows), left, NT)[:1]
        base_ref[b : b + 1, :] = state_rows[b] + section_step * (source_ref[b : b + 1, :] - state_image)


def shared_kernel(
    index_ref,
    count_ref,
    facts_ref,
    inner_ref,
    outer_ref,
    coupling_ref,
    _partial_in_ref,
    _base_in_ref,
    partial_ref,
    rhs_ref,
    image_ref,
    sums_ref,
):
    blocks, block, _ = image_ref.shape
    odd, first, last = (facts_ref[i] == 1 for i in range(3))
    inner_state = state_of(inner_ref, HALO * block, HALO)
    outer_state = state_of(outer_ref, HALO * block, HALO)
    lower_state = jnp.where(first, 0.0, jnp.where(odd, inner_state, outer_state))
    upper_state = jnp.where(last, 0.0, jnp.where(odd, outer_state, inner_state))
    nothing = jnp.zeros((block, block), BF16)

    def lower(pick):
        picked = jnp.where(odd, block_of(inner_ref, pick, block), block_of(outer_ref, pick, block))
        return jnp.where(first, nothing, picked)

    def upper(pick):
        picked = jnp.where(odd, block_of(outer_ref, pick, block), block_of(inner_ref, pick, block))
        return jnp.where(last, nothing, picked)

    def chosen(rows, pick):
        row = rows[:1]
        for i in range(1, HALO):
            row = jnp.where(pick == i, rows[i : i + 1], row)
        return row

    @pl.when(facts_ref[3] > 0)
    def _():
        for b in range(blocks):
            for s in range(2, coupling_ref.shape[1]):
                pick = index_ref[b, s]
                above = pick - HALO - blocks

                @pl.when((count_ref[b] > s) & ((pick < HALO) | (above >= 0)))
                def _(b=b, s=s, pick=pick, above=above):
                    at = jnp.where(above >= 0, above, pick)
                    picked = jnp.where(above >= 0, upper(at), lower(at))
                    row = jnp.where(above >= 0, chosen(upper_state, at), chosen(lower_state, at))
                    left = coupling_ref[b, s]
                    partial_ref[b] += dot(left, picked, NN)
                    rhs_ref[b : b + 1, :] -= section_step * dot(stack_rows([row]), left, NT)[:1]

    images, rows_of = [], []
    for b in range(blocks):
        below, above = index_ref[b, 0], index_ref[b, 1] - HALO - blocks
        left = jnp.concatenate([coupling_ref[b, 0], coupling_ref[b, 1]], axis=1)
        right = jnp.concatenate([lower(below), upper(above)], axis=0)
        image = (partial_ref[b] + dot(left, right, NN)).astype(BF16)
        rows = stack_rows([chosen(lower_state, below), chosen(upper_state, above)])
        rhs = rhs_ref[b : b + 1, :] - section_step * dot(rows, left, NT)[:1]
        image_ref[b] = image
        rhs_ref[b : b + 1, :] = rhs
        images.append(image)
        rows_of.append(split_rows(rhs, 3))
    image = jnp.concatenate(images, axis=0)
    gram = dot(image, image, TN)
    moment = dot(jnp.concatenate(rows_of, axis=1), image, NN)
    half = block // 2
    top, bottom = gram[:half], gram[half:]
    sub = lax.broadcasted_iota(jnp.int32, (half, block), 0)
    lane = lax.broadcasted_iota(jnp.int32, (half, block), 1)
    sums_ref[:half] = jnp.where(lane < sub, pltpu.roll(bottom, half, 1), top)
    pivots = jnp.where(lane == sub, top, jnp.where(lane == sub + half, bottom, 0.0))
    pivots = jnp.sum(pivots, axis=0, keepdims=True)
    row = lax.broadcasted_iota(jnp.int32, (8, block), 0)
    total = jnp.sum(moment, axis=0, keepdims=True)
    sums_ref[half:] = jnp.where(row == 0, pivots, jnp.where(row == 1, total, 0.0))


def spread(value, shape):
    return jnp.broadcast_to(value, shape)


def eliminate(rows, wide_ref, pair_ref):
    order = rows[0].shape[1]
    panels = len(rows)
    rows = list(rows)
    shape = (PANEL, order)
    lane = lax.broadcasted_iota(jnp.int32, shape, 1)
    sub = lax.broadcasted_iota(jnp.int32, shape, 0)

    def update(q, c, solved):
        terms = [spread(rows[q][:, c + k : c + k + 1], shape) * solved[k] for k in range(PANEL)]
        while len(terms) > 1:
            terms = [x + y for x, y in zip(terms[::2], terms[1::2])]
        rows[q] = jnp.where((lane >= c) & (lane < c + PANEL), 0.0, rows[q]) - terms[0]

    done = []
    waiting = []
    for p in range(panels):
        c = p * PANEL
        panel = (lane >= c) & (lane < c + PANEL)
        columns = [spread(rows[p][:, c + j : c + j + 1], shape) for j in range(PANEL)]
        at = p % 2 * PANEL
        wide_ref[at : at + PANEL, :] = jnp.where(panel, 0.0, rows[p])
        for j in range(PANEL):
            base = (at + j) * PANEL
            pair_ref[base : base + PANEL, :] = columns[j]
        wide = [spread(wide_ref[at + i : at + i + 1, :], shape) for i in range(PANEL)]
        a = [
            [
                spread(pair_ref[(at + j) * PANEL + i : (at + j) * PANEL + i + 1, :], shape) if j >= i else None
                for j in range(PANEL)
            ]
            for i in range(PANEL)
        ]
        out = jnp.zeros(shape, F32)
        solved = [None] * PANEL
        for k in range(PANEL):
            pivot = a[k][k]
            root = lax.rsqrt(pivot)
            if k % 2 == 0:
                inv = pl.reciprocal(pivot, approx=True)
                minor = pivot * a[k + 1][k + 1] - a[k][k + 1] * a[k][k + 1]
                next_inv = pivot * pl.reciprocal(minor, approx=True)
            else:
                inv = next_inv
            unit = jnp.where(lane == c + k, 1.0, wide[k])
            out = jnp.where(sub == k, unit * root, out)
            solved[k] = unit * inv
            factor = [None] * PANEL
            for j in range(k + 1, PANEL):
                factor[j] = a[k][j] * inv
            for i in range(k + 1, PANEL):
                for j in range(i, PANEL):
                    a[i][j] = a[i][j] - factor[i] * a[k][j]
                wide[i] = wide[i] - factor[i] * unit
            for i in range(k):
                for j in range(k + 1, PANEL):
                    a[i][j] = a[i][j] - a[i][k] * factor[j]
                solved[i] = solved[i] - a[i][k] * solved[k]
            for j in range(k + 1, PANEL):
                a[k][j] = factor[j]
            share = pl.cdiv(len(waiting), PANEL - k)
            for job in waiting[:share]:
                update(*job)
            waiting = waiting[share:]
        if p + 1 < panels:
            update(p + 1, c, solved)
        waiting = [(q, c, solved) for q in range(p + 2, panels)]
        done.append(jnp.where(lane <= c + sub, out, 0.0))
    return done


def finish_kernel(*refs, rows_total):
    sum_refs = refs[:-11]
    image_ref, packed_ref, rhs_ref, new_ref, new_image_ref, guess_ref, residual_ref = refs[-11:-4]
    gram_ref, factor_ref, wide_ref, pair_ref = refs[-4:]
    blocks, block, _ = image_ref.shape
    half = block // 2
    packed = sum_refs[0][...]
    for ref in sum_refs[1:]:
        packed = packed + ref[...]
    top, pivots = packed[:half], packed[half : half + 1]
    sub = lax.broadcasted_iota(jnp.int32, (half, block), 0)
    lane = lax.broadcasted_iota(jnp.int32, (half, block), 1)
    upper = jnp.where(lane >= sub, top, 0.0)
    lower = jnp.where((lane >= half) & (lane < sub + half), pltpu.roll(top, half, 1), 0.0)
    lower = jnp.where(lane == sub + half, pivots, lower)
    once = jnp.concatenate([upper, lower], axis=0)
    row = lax.broadcasted_iota(jnp.int32, (block, block), 0)
    col = lax.broadcasted_iota(jnp.int32, (block, block), 1)
    across = lax.rsqrt(pivots)
    half_scaled = (once * across).T * across
    gram_ref[...] = half_scaled + jnp.where(row == col, 0.0, half_scaled.T)
    done = eliminate([gram_ref[p : p + PANEL, :] for p in range(0, block, PANEL)], wide_ref, pair_ref)
    for p, panel in enumerate(done):
        factor_ref[p * PANEL : (p + 1) * PANEL, :] = panel
    factor = factor_ref[...] * (across * rows_total**0.5)
    moment = packed[half + 1 : half + 2] * (1.0 / rows_total)
    coefficients = jnp.sum(factor * moment, axis=1, keepdims=True)
    weights = jnp.sum(factor * coefficients, axis=0, keepdims=True)
    weights = split_rows(weights, 3)
    high = factor.astype(BF16)
    low = (factor - high.astype(F32)).astype(BF16)
    both = jnp.concatenate([high, low], axis=1)
    image = image_ref[...].reshape(blocks * block, block)
    basis = packed_ref[: blocks * block]
    new_image = dot(jnp.concatenate([image, image], axis=1), both, NT)
    new_image_ref[...] = new_image.astype(BF16).reshape(new_image_ref.shape)
    new_basis = dot(jnp.concatenate([basis, basis], axis=1), both, NT)
    new_ref[...] = new_basis.astype(BF16).reshape(new_ref.shape)
    guess = jnp.sum(dot(weights, basis, NT), axis=0, keepdims=True)
    fitted = jnp.sum(dot(weights, image, NT), axis=0, keepdims=True)
    for b in range(blocks):
        part = slice(b * block, (b + 1) * block)
        guess_ref[b : b + 1, :] = guess[:, part]
        residual_ref[b : b + 1, :] = rhs_ref[b : b + 1, :] - fitted[:, part]


def near(*arrays):
    return [pltpu.with_memory_space_constraint(array, pltpu.VMEM) for array in arrays]


def far(*arrays):
    return [pltpu.with_memory_space_constraint(array, pltpu.HBM) for array in arrays]


def vmem():
    return pl.BlockSpec(memory_space=pltpu.VMEM)


def smem():
    return pl.BlockSpec(memory_space=pltpu.SMEM)


def pack(basis, state):
    blocks, block, columns = basis.shape
    rows = blocks * block
    return pl.pallas_call(
        pack_kernel,
        out_shape=pltpu.VMEM((rows + 16 * pl.cdiv(blocks, 16), columns), BF16),
        in_specs=[pl.BlockSpec(memory_space=pl.ANY)] * 2,
        out_specs=vmem(),
        scratch_shapes=[pltpu.VMEM(state.shape, BF16), pltpu.SemaphoreType.DMA((2,))],
        compiler_params=pltpu.CompilerParams(vmem_limit_bytes=VMEM_LIMIT),
        name="pack",
    )(*far(basis.reshape(rows, columns), state))


def swap_pairs(parity, groups, devices):
    pairs = []
    for group in range(groups):
        for device in range(devices):
            other = device + 1 if device % 2 == parity else device - 1
            if 0 <= other < devices:
                pairs.append((group * devices + device, group * devices + other))
            else:
                twin = group ^ 1 if group ^ 1 < groups else group
                pairs.append((group * devices + device, twin * devices + device))
    return pairs


def halo(packed, basis, state):
    groups, devices = (lax.axis_size(axis) for axis in AXES)
    odd = lax.axis_index("dom") % 2
    got = []
    for parity in (1, 0):
        sent = packed
        if basis.shape[0] > HALO:
            up = odd == parity
            sent = pack(*(jnp.where(up, whole[-HALO:], whole[:HALO]) for whole in (basis, state)))
        got.append(lax.ppermute(sent, AXES, swap_pairs(parity, groups, devices)))
    return got


def exchange_stages(sizes):
    group, dom = sizes
    dom_bits = [1 << i for i in range(dom.bit_length() - 1)]
    group_bits = [dom << i for i in range(group.bit_length() - 1)]
    bits = group_bits[:1] + dom_bits[1:2] + dom_bits[2:] + group_bits[1:]
    stages = [dom_bits[:1], bits[:2] + [sum(bits[:2])], *([bit] for bit in bits[2:])]
    if len(dom_bits) < 2 or not group_bits:
        stages = [dom_bits[:1], *([bit] for bit in bits)]
    return stages[:1] + [[bit | 1 for bit in stage] for stage in stages[1:]]


def sum_parts(values):
    sizes = [lax.axis_size(axis) for axis in AXES]
    devices = sizes[0] * sizes[1]
    if any(size & (size - 1) for size in sizes):
        return [lax.psum(values, AXES)]
    parts = [values]
    for stage in exchange_stages(sizes):
        total = functools.reduce(jnp.add, parts)
        parts = [total]
        for bit in stage:
            pairs = [(i, i ^ bit) for i in range(devices)]
            parts.append(lax.ppermute(total, AXES, pairs))
    return parts


def finish(parts, image, packed, rhs, rows_total):
    blocks, block, columns = image.shape
    return pl.pallas_call(
        functools.partial(finish_kernel, rows_total=rows_total),
        out_shape=(
            jax.ShapeDtypeStruct(image.shape, BF16),
            jax.ShapeDtypeStruct(image.shape, BF16),
            jax.ShapeDtypeStruct(rhs.shape, F32),
            jax.ShapeDtypeStruct(rhs.shape, F32),
        ),
        in_specs=[vmem()] * (len(parts) + 3),
        out_specs=(vmem(),) * 4,
        scratch_shapes=[pltpu.VMEM((block, columns), F32)] * 2 + [pltpu.VMEM((2 * PANEL, columns), F32), pltpu.VMEM((2 * PANEL * PANEL, columns), F32)],
        compiler_params=pltpu.CompilerParams(vmem_limit_bytes=VMEM_LIMIT),
        name="finish",
    )(*near(*parts, image, packed, rhs))


def body(prior_basis, section_state, source, diag_blocks, coupling, neighbour_index, slot_count):
    blocks, block, columns = prior_basis.shape
    packed = pack(prior_basis, section_state)
    outer, inner = halo(packed, prior_basis, section_state)
    partial, base, near_coupling, *near_scalars = pl.pallas_call(
        local_kernel,
        out_shape=(
            pltpu.VMEM(prior_basis.shape, F32),
            pltpu.VMEM(source.shape, F32),
            pltpu.VMEM(coupling.shape, BF16),
            pltpu.SMEM(neighbour_index.shape, jnp.int32),
            pltpu.SMEM(slot_count.shape, jnp.int32),
            pltpu.SMEM((4,), jnp.int32),
        ),
        in_specs=[smem()] * 2 + [vmem()] * 3 + [pl.BlockSpec(memory_space=pl.ANY)],
        out_specs=(vmem(),) * 3 + (smem(),) * 3,
        scratch_shapes=[pltpu.SemaphoreType.DMA],
        compiler_params=pltpu.CompilerParams(vmem_limit_bytes=VMEM_LIMIT),
        name="local_part",
    )(*far(neighbour_index, slot_count), *near(packed), *far(source, diag_blocks, coupling))
    _, rhs, image, sums = pl.pallas_call(
        shared_kernel,
        out_shape=(
            pltpu.VMEM(prior_basis.shape, F32),
            pltpu.VMEM(source.shape, F32),
            pltpu.VMEM(prior_basis.shape, BF16),
            pltpu.VMEM((block // 2 + 8, columns), F32),
        ),
        in_specs=[smem()] * 3 + [vmem()] * 5,
        out_specs=(vmem(),) * 4,
        input_output_aliases={6: 0, 7: 1},
        compiler_params=pltpu.CompilerParams(vmem_limit_bytes=VMEM_LIMIT),
        name="shared_part",
    )(
        *(pltpu.with_memory_space_constraint(array, pltpu.SMEM) for array in near_scalars),
        *near(inner, outer, near_coupling, partial, base),
    )
    parts = sum_parts(sums)
    rows_total = blocks * block * lax.axis_size("group") * lax.axis_size("dom")
    return finish(parts, image, packed, rhs, float(rows_total))


def solution(mesh):
    rows = P(AXES, None)
    cubes = P(AXES, None, None)
    return jax.shard_map(
        body,
        mesh=mesh,
        in_specs=(cubes, rows, rows, cubes, P(AXES, None, None, None), rows, P(AXES)),
        out_specs=(cubes, cubes, rows, rows),
        check_vma=False,
    )
```

```python
import functools

import jax
import jax.numpy as jnp
from jax import lax
from jax.experimental import pallas as pl
from jax.experimental.pallas import tpu as pltpu
from jax.sharding import PartitionSpec as P

HALO = 4
PANEL = 8
PACK_COPIES = 4
VMEM_LIMIT = 16 << 20
section_step = 0.25
AXES = ("group", "dom")
F32 = jnp.float32
BF16 = jnp.bfloat16

NN = (((1,), (0,)), ((), ()))
NT = (((1,), (1,)), ((), ()))
TN = (((0,), (0,)), ((), ()))


def dot(a, b, dims):
    return lax.dot_general(a, b, dims, preferred_element_type=F32)


def split_rows(row, count):
    sub = lax.broadcasted_iota(jnp.int32, (16, row.shape[1]), 0)
    rows = jnp.zeros((16, row.shape[1]), F32)
    rest = row
    for part in range(count):
        piece = rest.astype(BF16).astype(F32)
        rows = jnp.where(sub == part, piece, rows)
        rest = rest - piece
    return rows.astype(BF16)


def stack_rows(rows):
    return jnp.concatenate([jnp.broadcast_to(row, (16, row.shape[1])) for row in rows], axis=1).astype(BF16)


def pack_kernel(basis_ref, state_ref, packed_ref, rows_ref, sems):
    rows = basis_ref.shape[0]
    state_copy = pltpu.make_async_copy(state_ref, rows_ref, sems.at[0])
    state_copy.start()
    share = rows // PACK_COPIES
    copies = []
    for part in range(PACK_COPIES):
        at = pl.ds(part * share, share)
        copies.append(pltpu.make_async_copy(basis_ref.at[at], packed_ref.at[at], sems.at[part + 1]))
        copies[-1].start()
    state_copy.wait()
    state = rows_ref[...].astype(F32)
    spare = jnp.zeros((packed_ref.shape[0] - rows - state.shape[0], state.shape[1]), F32)
    packed_ref[rows:] = jnp.concatenate([state, spare], axis=0).astype(BF16)
    for copy in copies:
        copy.wait()


def state_of(packed_ref, rows, count):
    return packed_ref[rows:].astype(F32)[:count]


def block_of(packed_ref, pick, block):
    return packed_ref[pl.ds(pl.multiple_of(pick * block, block), block)]


def local_kernel(
    index_ref,
    count_ref,
    packed_ref,
    source_ref,
    diag_ref,
    coupling_ref,
    partial_ref,
    base_ref,
    near_coupling_ref,
    near_index_ref,
    near_count_ref,
    facts_ref,
    sem,
):
    copy = pltpu.make_async_copy(coupling_ref, near_coupling_ref, sem)
    copy.start()
    blocks, block, _ = diag_ref.shape
    slots = coupling_ref.shape[1]
    here = lax.axis_index("dom")
    facts_ref[0] = here % 2
    facts_ref[1] = (here == 0).astype(jnp.int32)
    facts_ref[2] = (here == lax.axis_size("dom") - 1).astype(jnp.int32)
    shared = jnp.int32(0)
    for b in range(blocks):
        near_count_ref[b] = count_ref[b]
        for s in range(slots):
            near_index_ref[b, s] = index_ref[b, s]
        for s in range(2, slots):
            outside = (index_ref[b, s] < HALO) | (index_ref[b, s] >= HALO + blocks)
            shared += ((count_ref[b] > s) & outside).astype(jnp.int32)
    facts_ref[3] = shared
    state = state_of(packed_ref, blocks * block, blocks)
    state_rows = [state[b : b + 1] for b in range(blocks)]
    copy.wait()
    for b in range(blocks):
        left, right, rows = [diag_ref[b]], [block_of(packed_ref, b, block)], [state_rows[b]]
        for s in range(2, slots):
            pick = index_ref[b, s] - HALO
            live = (count_ref[b] > s) & (pick >= 0) & (pick < blocks)
            pick = jnp.clip(pick, 0, blocks - 1)
            left.append(near_coupling_ref[b, s])
            right.append(jnp.where(live, block_of(packed_ref, pick, block), jnp.zeros((block, block), BF16)))
            row = state_rows[0]
            for i in range(1, blocks):
                row = jnp.where(pick == i, state_rows[i], row)
            rows.append(jnp.where(live, row, 0.0))
        left = jnp.concatenate(left, axis=1)
        partial_ref[b] = dot(left, jnp.concatenate(right, axis=0), NN)
        state_image = dot(stack_rows(rows), left, NT)[:1]
        base_ref[b : b + 1, :] = state_rows[b] + section_step * (source_ref[b : b + 1, :] - state_image)


def shared_kernel(
    index_ref,
    count_ref,
    facts_ref,
    inner_ref,
    outer_ref,
    coupling_ref,
    _partial_in_ref,
    _base_in_ref,
    partial_ref,
    rhs_ref,
    image_ref,
    sums_ref,
):
    blocks, block, _ = image_ref.shape
    odd, first, last = (facts_ref[i] == 1 for i in range(3))
    inner_state = state_of(inner_ref, HALO * block, HALO)
    outer_state = state_of(outer_ref, HALO * block, HALO)
    lower_state = jnp.where(first, 0.0, jnp.where(odd, inner_state, outer_state))
    upper_state = jnp.where(last, 0.0, jnp.where(odd, outer_state, inner_state))
    nothing = jnp.zeros((block, block), BF16)

    def lower(pick):
        picked = jnp.where(odd, block_of(inner_ref, pick, block), block_of(outer_ref, pick, block))
        return jnp.where(first, nothing, picked)

    def upper(pick):
        picked = jnp.where(odd, block_of(outer_ref, pick, block), block_of(inner_ref, pick, block))
        return jnp.where(last, nothing, picked)

    def chosen(rows, pick):
        row = rows[:1]
        for i in range(1, HALO):
            row = jnp.where(pick == i, rows[i : i + 1], row)
        return row

    @pl.when(facts_ref[3] > 0)
    def _():
        for b in range(blocks):
            for s in range(2, coupling_ref.shape[1]):
                pick = index_ref[b, s]
                above = pick - HALO - blocks

                @pl.when((count_ref[b] > s) & ((pick < HALO) | (above >= 0)))
                def _(b=b, s=s, pick=pick, above=above):
                    at = jnp.where(above >= 0, above, pick)
                    picked = jnp.where(above >= 0, upper(at), lower(at))
                    row = jnp.where(above >= 0, chosen(upper_state, at), chosen(lower_state, at))
                    left = coupling_ref[b, s]
                    partial_ref[b] += dot(left, picked, NN)
                    rhs_ref[b : b + 1, :] -= section_step * dot(stack_rows([row]), left, NT)[:1]

    images, rows_of = [], []
    for b in range(blocks):
        below, above = index_ref[b, 0], index_ref[b, 1] - HALO - blocks
        left = jnp.concatenate([coupling_ref[b, 0], coupling_ref[b, 1]], axis=1)
        right = jnp.concatenate([lower(below), upper(above)], axis=0)
        image = (partial_ref[b] + dot(left, right, NN)).astype(BF16)
        rows = stack_rows([chosen(lower_state, below), chosen(upper_state, above)])
        rhs = rhs_ref[b : b + 1, :] - section_step * dot(rows, left, NT)[:1]
        image_ref[b] = image
        rhs_ref[b : b + 1, :] = rhs
        images.append(image)
        rows_of.append(split_rows(rhs, 3))
    image = jnp.concatenate(images, axis=0)
    gram = dot(image, image, TN)
    moment = dot(jnp.concatenate(rows_of, axis=1), image, NN)
    half = block // 2
    top, bottom = gram[:half], gram[half:]
    sub = lax.broadcasted_iota(jnp.int32, (half, block), 0)
    lane = lax.broadcasted_iota(jnp.int32, (half, block), 1)
    sums_ref[:half] = jnp.where(lane < sub, pltpu.roll(bottom, half, 1), top)
    pivots = jnp.where(lane == sub, top, jnp.where(lane == sub + half, bottom, 0.0))
    pivots = jnp.sum(pivots, axis=0, keepdims=True)
    row = lax.broadcasted_iota(jnp.int32, (8, block), 0)
    total = jnp.sum(moment, axis=0, keepdims=True)
    sums_ref[half:] = jnp.where(row == 0, pivots, jnp.where(row == 1, total, 0.0))


def spread(value, shape):
    return jnp.broadcast_to(value, shape)


def eliminate(rows, wide_ref, pair_ref):
    order = rows[0].shape[1]
    panels = len(rows)
    rows = list(rows)
    shape = (PANEL, order)
    lane = lax.broadcasted_iota(jnp.int32, shape, 1)
    sub = lax.broadcasted_iota(jnp.int32, shape, 0)

    def update(q, c, solved):
        terms = [spread(rows[q][:, c + k : c + k + 1], shape) * solved[k] for k in range(PANEL)]
        while len(terms) > 1:
            terms = [x + y for x, y in zip(terms[::2], terms[1::2])]
        rows[q] = jnp.where((lane >= c) & (lane < c + PANEL), 0.0, rows[q]) - terms[0]

    done = []
    waiting = []
    for p in range(panels):
        c = p * PANEL
        panel = (lane >= c) & (lane < c + PANEL)
        columns = [spread(rows[p][:, c + j : c + j + 1], shape) for j in range(PANEL)]
        at = p % 2 * PANEL
        wide_ref[at : at + PANEL, :] = jnp.where(panel, 0.0, rows[p])
        for j in range(PANEL):
            base = (at + j) * PANEL
            pair_ref[base : base + PANEL, :] = columns[j]
        wide = [spread(wide_ref[at + i : at + i + 1, :], shape) for i in range(PANEL)]
        a = [
            [
                spread(pair_ref[(at + j) * PANEL + i : (at + j) * PANEL + i + 1, :], shape) if j >= i else None
                for j in range(PANEL)
            ]
            for i in range(PANEL)
        ]
        out = jnp.zeros(shape, F32)
        solved = [None] * PANEL
        for k in range(PANEL):
            pivot = a[k][k]
            root = lax.rsqrt(pivot)
            if k % 2 == 0:
                inv = pl.reciprocal(pivot, approx=True)
                minor = pivot * a[k + 1][k + 1] - a[k][k + 1] * a[k][k + 1]
                next_inv = pivot * pl.reciprocal(minor, approx=True)
            else:
                inv = next_inv
            unit = jnp.where(lane == c + k, 1.0, wide[k])
            out = jnp.where(sub == k, unit * root, out)
            solved[k] = unit * inv
            factor = [None] * PANEL
            for j in range(k + 1, PANEL):
                factor[j] = a[k][j] * inv
            for i in range(k + 1, PANEL):
                for j in range(i, PANEL):
                    a[i][j] = a[i][j] - factor[i] * a[k][j]
                wide[i] = wide[i] - factor[i] * unit
            for i in range(k):
                for j in range(k + 1, PANEL):
                    a[i][j] = a[i][j] - a[i][k] * factor[j]
                solved[i] = solved[i] - a[i][k] * solved[k]
            for j in range(k + 1, PANEL):
                a[k][j] = factor[j]
            share = pl.cdiv(len(waiting), PANEL - k)
            for job in waiting[:share]:
                update(*job)
            waiting = waiting[share:]
        if p + 1 < panels:
            update(p + 1, c, solved)
        waiting = [(q, c, solved) for q in range(p + 2, panels)]
        done.append(jnp.where(lane <= c + sub, out, 0.0))
    return done


def finish_kernel(*refs, rows_total):
    sum_refs = refs[:-11]
    image_ref, packed_ref, rhs_ref, new_ref, new_image_ref, guess_ref, residual_ref = refs[-11:-4]
    gram_ref, factor_ref, wide_ref, pair_ref = refs[-4:]
    blocks, block, _ = image_ref.shape
    half = block // 2
    packed = sum_refs[0][...]
    for ref in sum_refs[1:]:
        packed = packed + ref[...]
    top, pivots = packed[:half], packed[half : half + 1]
    sub = lax.broadcasted_iota(jnp.int32, (half, block), 0)
    lane = lax.broadcasted_iota(jnp.int32, (half, block), 1)
    upper = jnp.where(lane >= sub, top, 0.0)
    lower = jnp.where((lane >= half) & (lane < sub + half), pltpu.roll(top, half, 1), 0.0)
    lower = jnp.where(lane == sub + half, pivots, lower)
    once = jnp.concatenate([upper, lower], axis=0)
    row = lax.broadcasted_iota(jnp.int32, (block, block), 0)
    col = lax.broadcasted_iota(jnp.int32, (block, block), 1)
    across = lax.rsqrt(pivots)
    half_scaled = (once * across).T * across
    gram_ref[...] = half_scaled + jnp.where(row == col, 0.0, half_scaled.T)
    done = eliminate([gram_ref[p : p + PANEL, :] for p in range(0, block, PANEL)], wide_ref, pair_ref)
    for p, panel in enumerate(done):
        factor_ref[p * PANEL : (p + 1) * PANEL, :] = panel
    factor = factor_ref[...] * (across * rows_total**0.5)
    moment = packed[half + 1 : half + 2] * (1.0 / rows_total)
    coefficients = jnp.sum(factor * moment, axis=1, keepdims=True)
    weights = jnp.sum(factor * coefficients, axis=0, keepdims=True)
    weights = split_rows(weights, 3)
    high = factor.astype(BF16)
    low = (factor - high.astype(F32)).astype(BF16)
    both = jnp.concatenate([high, low], axis=1)
    image = image_ref[...].reshape(blocks * block, block)
    basis = packed_ref[: blocks * block]
    new_image = dot(jnp.concatenate([image, image], axis=1), both, NT)
    new_image_ref[...] = new_image.astype(BF16).reshape(new_image_ref.shape)
    new_basis = dot(jnp.concatenate([basis, basis], axis=1), both, NT)
    new_ref[...] = new_basis.astype(BF16).reshape(new_ref.shape)
    guess = jnp.sum(dot(weights, basis, NT), axis=0, keepdims=True)
    fitted = jnp.sum(dot(weights, image, NT), axis=0, keepdims=True)
    for b in range(blocks):
        part = slice(b * block, (b + 1) * block)
        guess_ref[b : b + 1, :] = guess[:, part]
        residual_ref[b : b + 1, :] = rhs_ref[b : b + 1, :] - fitted[:, part]


def near(*arrays):
    return [pltpu.with_memory_space_constraint(array, pltpu.VMEM) for array in arrays]


def far(*arrays):
    return [pltpu.with_memory_space_constraint(array, pltpu.HBM) for array in arrays]


def vmem():
    return pl.BlockSpec(memory_space=pltpu.VMEM)


def smem():
    return pl.BlockSpec(memory_space=pltpu.SMEM)


def pack(basis, state):
    blocks, block, columns = basis.shape
    rows = blocks * block
    return pl.pallas_call(
        pack_kernel,
        out_shape=pltpu.VMEM((rows + 16 * pl.cdiv(blocks, 16), columns), BF16),
        in_specs=[pl.BlockSpec(memory_space=pl.ANY)] * 2,
        out_specs=vmem(),
        scratch_shapes=[pltpu.VMEM(state.shape, BF16), pltpu.SemaphoreType.DMA((PACK_COPIES + 1,))],
        compiler_params=pltpu.CompilerParams(vmem_limit_bytes=VMEM_LIMIT),
        name="pack",
    )(*far(basis.reshape(rows, columns), state))


def swap_pairs(parity, groups, devices):
    pairs = []
    for group in range(groups):
        for device in range(devices):
            other = device + 1 if device % 2 == parity else device - 1
            if 0 <= other < devices:
                pairs.append((group * devices + device, group * devices + other))
            else:
                twin = group ^ 1 if group ^ 1 < groups else group
                pairs.append((group * devices + device, twin * devices + device))
    return pairs


def halo(packed, basis, state):
    groups, devices = (lax.axis_size(axis) for axis in AXES)
    odd = lax.axis_index("dom") % 2
    got = []
    for parity in (1, 0):
        sent = packed
        if basis.shape[0] > HALO:
            up = odd == parity
            sent = pack(*(jnp.where(up, whole[-HALO:], whole[:HALO]) for whole in (basis, state)))
        got.append(lax.ppermute(sent, AXES, swap_pairs(parity, groups, devices)))
    return got


def exchange_stages(sizes):
    group, dom = sizes
    dom_bits = [1 << i for i in range(dom.bit_length() - 1)]
    group_bits = [dom << i for i in range(group.bit_length() - 1)]
    bits = group_bits[:1] + dom_bits[1:2] + dom_bits[2:] + group_bits[1:]
    stages = [dom_bits[:1], bits[:2] + [sum(bits[:2])], *([bit] for bit in bits[2:])]
    if len(dom_bits) < 2 or not group_bits:
        stages = [dom_bits[:1], *([bit] for bit in bits)]
    return stages[:1] + [[bit | 1 for bit in stage] for stage in stages[1:]]


def sum_parts(values):
    sizes = [lax.axis_size(axis) for axis in AXES]
    devices = sizes[0] * sizes[1]
    if any(size & (size - 1) for size in sizes):
        return [lax.psum(values, AXES)]
    parts = [values]
    for stage in exchange_stages(sizes):
        total = functools.reduce(jnp.add, parts)
        parts = [total]
        for bit in stage:
            pairs = [(i, i ^ bit) for i in range(devices)]
            parts.append(lax.ppermute(total, AXES, pairs))
    return parts


def finish(parts, image, packed, rhs, rows_total):
    blocks, block, columns = image.shape
    return pl.pallas_call(
        functools.partial(finish_kernel, rows_total=rows_total),
        out_shape=(
            jax.ShapeDtypeStruct(image.shape, BF16),
            jax.ShapeDtypeStruct(image.shape, BF16),
            jax.ShapeDtypeStruct(rhs.shape, F32),
            jax.ShapeDtypeStruct(rhs.shape, F32),
        ),
        in_specs=[vmem()] * (len(parts) + 3),
        out_specs=(vmem(),) * 4,
        scratch_shapes=[pltpu.VMEM((block, columns), F32)] * 2 + [pltpu.VMEM((2 * PANEL, columns), F32), pltpu.VMEM((2 * PANEL * PANEL, columns), F32)],
        compiler_params=pltpu.CompilerParams(vmem_limit_bytes=VMEM_LIMIT),
        name="finish",
    )(*near(*parts, image, packed, rhs))


def body(prior_basis, section_state, source, diag_blocks, coupling, neighbour_index, slot_count):
    blocks, block, columns = prior_basis.shape
    packed = pack(prior_basis, section_state)
    outer, inner = halo(packed, prior_basis, section_state)
    partial, base, near_coupling, *near_scalars = pl.pallas_call(
        local_kernel,
        out_shape=(
            pltpu.VMEM(prior_basis.shape, F32),
            pltpu.VMEM(source.shape, F32),
            pltpu.VMEM(coupling.shape, BF16),
            pltpu.SMEM(neighbour_index.shape, jnp.int32),
            pltpu.SMEM(slot_count.shape, jnp.int32),
            pltpu.SMEM((4,), jnp.int32),
        ),
        in_specs=[smem()] * 2 + [vmem()] * 3 + [pl.BlockSpec(memory_space=pl.ANY)],
        out_specs=(vmem(),) * 3 + (smem(),) * 3,
        scratch_shapes=[pltpu.SemaphoreType.DMA],
        compiler_params=pltpu.CompilerParams(vmem_limit_bytes=VMEM_LIMIT),
        name="local_part",
    )(*far(neighbour_index, slot_count), *near(packed), *far(source, diag_blocks, coupling))
    _, rhs, image, sums = pl.pallas_call(
        shared_kernel,
        out_shape=(
            pltpu.VMEM(prior_basis.shape, F32),
            pltpu.VMEM(source.shape, F32),
            pltpu.VMEM(prior_basis.shape, BF16),
            pltpu.VMEM((block // 2 + 8, columns), F32),
        ),
        in_specs=[smem()] * 3 + [vmem()] * 5,
        out_specs=(vmem(),) * 4,
        input_output_aliases={6: 0, 7: 1},
        compiler_params=pltpu.CompilerParams(vmem_limit_bytes=VMEM_LIMIT),
        name="shared_part",
    )(
        *(pltpu.with_memory_space_constraint(array, pltpu.SMEM) for array in near_scalars),
        *near(inner, outer, near_coupling, partial, base),
    )
    parts = sum_parts(sums)
    rows_total = blocks * block * lax.axis_size("group") * lax.axis_size("dom")
    return finish(parts, image, packed, rhs, float(rows_total))


def solution(mesh):
    rows = P(AXES, None)
    cubes = P(AXES, None, None)
    return jax.shard_map(
        body,
        mesh=mesh,
        in_specs=(cubes, rows, rows, cubes, P(AXES, None, None, None), rows, P(AXES)),
        out_specs=(cubes, cubes, rows, rows),
        check_vma=False,
    )
```

```python
import functools

import jax
import jax.numpy as jnp
from jax import lax
from jax.experimental import pallas as pl
from jax.experimental.pallas import tpu as pltpu
from jax.sharding import PartitionSpec as P

HALO = 4
PANEL = 8
PACK_COPIES = 4
VMEM_LIMIT = 16 << 20
section_step = 0.25
AXES = ("group", "dom")
F32 = jnp.float32
BF16 = jnp.bfloat16

NN = (((1,), (0,)), ((), ()))
NT = (((1,), (1,)), ((), ()))
TN = (((0,), (0,)), ((), ()))


def dot(a, b, dims):
    return lax.dot_general(a, b, dims, preferred_element_type=F32)


def split_rows(row, count):
    sub = lax.broadcasted_iota(jnp.int32, (16, row.shape[1]), 0)
    rows = jnp.zeros((16, row.shape[1]), F32)
    rest = row
    for part in range(count):
        piece = rest.astype(BF16).astype(F32)
        rows = jnp.where(sub == part, piece, rows)
        rest = rest - piece
    return rows.astype(BF16)


def stack_rows(rows):
    return jnp.concatenate([jnp.broadcast_to(row, (16, row.shape[1])) for row in rows], axis=1).astype(BF16)


def pack_kernel(basis_ref, state_ref, packed_ref, rows_ref, sems):
    rows = basis_ref.shape[0]
    share = rows // PACK_COPIES
    copies = []
    for part in range(PACK_COPIES):
        at = pl.ds(part * share, share)
        copies.append(pltpu.make_async_copy(basis_ref.at[at], packed_ref.at[at], sems.at[part + 1]))
        copies[-1].start()
    state_copy = pltpu.make_async_copy(state_ref, rows_ref, sems.at[0])
    state_copy.start()
    state_copy.wait()
    state = rows_ref[...].astype(F32)
    spare = jnp.zeros((packed_ref.shape[0] - rows - state.shape[0], state.shape[1]), F32)
    packed_ref[rows:] = jnp.concatenate([state, spare], axis=0).astype(BF16)
    for copy in copies:
        copy.wait()


def state_of(packed_ref, rows, count):
    return packed_ref[rows:].astype(F32)[:count]


def block_of(packed_ref, pick, block):
    return packed_ref[pl.ds(pl.multiple_of(pick * block, block), block)]


def local_kernel(
    index_ref,
    count_ref,
    packed_ref,
    source_ref,
    diag_ref,
    coupling_ref,
    partial_ref,
    base_ref,
    near_coupling_ref,
    near_index_ref,
    near_count_ref,
    facts_ref,
    sem,
):
    copy = pltpu.make_async_copy(coupling_ref, near_coupling_ref, sem)
    copy.start()
    blocks, block, _ = diag_ref.shape
    slots = coupling_ref.shape[1]
    here = lax.axis_index("dom")
    facts_ref[0] = here % 2
    facts_ref[1] = (here == 0).astype(jnp.int32)
    facts_ref[2] = (here == lax.axis_size("dom") - 1).astype(jnp.int32)
    shared = jnp.int32(0)
    for b in range(blocks):
        near_count_ref[b] = count_ref[b]
        for s in range(slots):
            near_index_ref[b, s] = index_ref[b, s]
        for s in range(2, slots):
            outside = (index_ref[b, s] < HALO) | (index_ref[b, s] >= HALO + blocks)
            shared += ((count_ref[b] > s) & outside).astype(jnp.int32)
    facts_ref[3] = shared
    state = state_of(packed_ref, blocks * block, blocks)
    state_rows = [state[b : b + 1] for b in range(blocks)]
    copy.wait()
    for b in range(blocks):
        left, right, rows = [diag_ref[b]], [block_of(packed_ref, b, block)], [state_rows[b]]
        for s in range(2, slots):
            pick = index_ref[b, s] - HALO
            live = (count_ref[b] > s) & (pick >= 0) & (pick < blocks)
            pick = jnp.clip(pick, 0, blocks - 1)
            left.append(near_coupling_ref[b, s])
            right.append(jnp.where(live, block_of(packed_ref, pick, block), jnp.zeros((block, block), BF16)))
            row = state_rows[0]
            for i in range(1, blocks):
                row = jnp.where(pick == i, state_rows[i], row)
            rows.append(jnp.where(live, row, 0.0))
        left = jnp.concatenate(left, axis=1)
        partial_ref[b] = dot(left, jnp.concatenate(right, axis=0), NN)
        state_image = dot(stack_rows(rows), left, NT)[:1]
        base_ref[b : b + 1, :] = state_rows[b] + section_step * (source_ref[b : b + 1, :] - state_image)


def shared_kernel(
    index_ref,
    count_ref,
    facts_ref,
    inner_ref,
    outer_ref,
    coupling_ref,
    _partial_in_ref,
    _base_in_ref,
    partial_ref,
    rhs_ref,
    image_ref,
    sums_ref,
):
    blocks, block, _ = image_ref.shape
    odd, first, last = (facts_ref[i] == 1 for i in range(3))
    inner_state = state_of(inner_ref, HALO * block, HALO)
    outer_state = state_of(outer_ref, HALO * block, HALO)
    lower_state = jnp.where(first, 0.0, jnp.where(odd, inner_state, outer_state))
    upper_state = jnp.where(last, 0.0, jnp.where(odd, outer_state, inner_state))
    nothing = jnp.zeros((block, block), BF16)

    def lower(pick):
        picked = jnp.where(odd, block_of(inner_ref, pick, block), block_of(outer_ref, pick, block))
        return jnp.where(first, nothing, picked)

    def upper(pick):
        picked = jnp.where(odd, block_of(outer_ref, pick, block), block_of(inner_ref, pick, block))
        return jnp.where(last, nothing, picked)

    def chosen(rows, pick):
        row = rows[:1]
        for i in range(1, HALO):
            row = jnp.where(pick == i, rows[i : i + 1], row)
        return row

    @pl.when(facts_ref[3] > 0)
    def _():
        for b in range(blocks):
            for s in range(2, coupling_ref.shape[1]):
                pick = index_ref[b, s]
                above = pick - HALO - blocks

                @pl.when((count_ref[b] > s) & ((pick < HALO) | (above >= 0)))
                def _(b=b, s=s, pick=pick, above=above):
                    at = jnp.where(above >= 0, above, pick)
                    picked = jnp.where(above >= 0, upper(at), lower(at))
                    row = jnp.where(above >= 0, chosen(upper_state, at), chosen(lower_state, at))
                    left = coupling_ref[b, s]
                    partial_ref[b] += dot(left, picked, NN)
                    rhs_ref[b : b + 1, :] -= section_step * dot(stack_rows([row]), left, NT)[:1]

    images, rows_of = [], []
    for b in range(blocks):
        below, above = index_ref[b, 0], index_ref[b, 1] - HALO - blocks
        left = jnp.concatenate([coupling_ref[b, 0], coupling_ref[b, 1]], axis=1)
        right = jnp.concatenate([lower(below), upper(above)], axis=0)
        image = (partial_ref[b] + dot(left, right, NN)).astype(BF16)
        rows = stack_rows([chosen(lower_state, below), chosen(upper_state, above)])
        rhs = rhs_ref[b : b + 1, :] - section_step * dot(rows, left, NT)[:1]
        image_ref[b] = image
        rhs_ref[b : b + 1, :] = rhs
        images.append(image)
        rows_of.append(split_rows(rhs, 3))
    image = jnp.concatenate(images, axis=0)
    gram = dot(image, image, TN)
    moment = dot(jnp.concatenate(rows_of, axis=1), image, NN)
    half = block // 2
    top, bottom = gram[:half], gram[half:]
    sub = lax.broadcasted_iota(jnp.int32, (half, block), 0)
    lane = lax.broadcasted_iota(jnp.int32, (half, block), 1)
    sums_ref[:half] = jnp.where(lane < sub, pltpu.roll(bottom, half, 1), top)
    pivots = jnp.where(lane == sub, top, jnp.where(lane == sub + half, bottom, 0.0))
    pivots = jnp.sum(pivots, axis=0, keepdims=True)
    row = lax.broadcasted_iota(jnp.int32, (8, block), 0)
    total = jnp.sum(moment, axis=0, keepdims=True)
    sums_ref[half:] = jnp.where(row == 0, pivots, jnp.where(row == 1, total, 0.0))


def spread(value, shape):
    return jnp.broadcast_to(value, shape)


def eliminate(rows, wide_ref, pair_ref):
    order = rows[0].shape[1]
    panels = len(rows)
    rows = list(rows)
    shape = (PANEL, order)
    lane = lax.broadcasted_iota(jnp.int32, shape, 1)
    sub = lax.broadcasted_iota(jnp.int32, shape, 0)

    def update(q, c, solved):
        terms = [spread(rows[q][:, c + k : c + k + 1], shape) * solved[k] for k in range(PANEL)]
        while len(terms) > 1:
            terms = [x + y for x, y in zip(terms[::2], terms[1::2])]
        rows[q] = jnp.where((lane >= c) & (lane < c + PANEL), 0.0, rows[q]) - terms[0]

    done = []
    waiting = []
    for p in range(panels):
        c = p * PANEL
        panel = (lane >= c) & (lane < c + PANEL)
        columns = [spread(rows[p][:, c + j : c + j + 1], shape) for j in range(PANEL)]
        at = p % 2 * PANEL
        wide_ref[at : at + PANEL, :] = jnp.where(panel, 0.0, rows[p])
        for j in range(PANEL):
            base = (at + j) * PANEL
            pair_ref[base : base + PANEL, :] = columns[j]
        wide = [spread(wide_ref[at + i : at + i + 1, :], shape) for i in range(PANEL)]
        a = [
            [
                spread(pair_ref[(at + j) * PANEL + i : (at + j) * PANEL + i + 1, :], shape) if j >= i else None
                for j in range(PANEL)
            ]
            for i in range(PANEL)
        ]
        out = jnp.zeros(shape, F32)
        solved = [None] * PANEL
        for k in range(PANEL):
            pivot = a[k][k]
            root = lax.rsqrt(pivot)
            if k % 2 == 0:
                inv = pl.reciprocal(pivot, approx=True)
                minor = pivot * a[k + 1][k + 1] - a[k][k + 1] * a[k][k + 1]
                next_inv = pivot * pl.reciprocal(minor, approx=True)
            else:
                inv = next_inv
            unit = jnp.where(lane == c + k, 1.0, wide[k])
            out = jnp.where(sub == k, unit * root, out)
            solved[k] = unit * inv
            factor = [None] * PANEL
            for j in range(k + 1, PANEL):
                factor[j] = a[k][j] * inv
            for i in range(k + 1, PANEL):
                for j in range(i, PANEL):
                    a[i][j] = a[i][j] - factor[i] * a[k][j]
                wide[i] = wide[i] - factor[i] * unit
            for i in range(k):
                for j in range(k + 1, PANEL):
                    a[i][j] = a[i][j] - a[i][k] * factor[j]
                solved[i] = solved[i] - a[i][k] * solved[k]
            for j in range(k + 1, PANEL):
                a[k][j] = factor[j]
            share = pl.cdiv(len(waiting), PANEL - k)
            for job in waiting[:share]:
                update(*job)
            waiting = waiting[share:]
        if p + 1 < panels:
            update(p + 1, c, solved)
        waiting = [(q, c, solved) for q in range(p + 2, panels)]
        done.append(jnp.where(lane <= c + sub, out, 0.0))
    return done


def finish_kernel(*refs, rows_total):
    sum_refs = refs[:-11]
    image_ref, packed_ref, rhs_ref, new_ref, new_image_ref, guess_ref, residual_ref = refs[-11:-4]
    gram_ref, factor_ref, wide_ref, pair_ref = refs[-4:]
    blocks, block, _ = image_ref.shape
    half = block // 2
    packed = sum_refs[0][...]
    for ref in sum_refs[1:]:
        packed = packed + ref[...]
    top, pivots = packed[:half], packed[half : half + 1]
    sub = lax.broadcasted_iota(jnp.int32, (half, block), 0)
    lane = lax.broadcasted_iota(jnp.int32, (half, block), 1)
    upper = jnp.where(lane >= sub, top, 0.0)
    lower = jnp.where((lane >= half) & (lane < sub + half), pltpu.roll(top, half, 1), 0.0)
    lower = jnp.where(lane == sub + half, pivots, lower)
    once = jnp.concatenate([upper, lower], axis=0)
    row = lax.broadcasted_iota(jnp.int32, (block, block), 0)
    col = lax.broadcasted_iota(jnp.int32, (block, block), 1)
    across = lax.rsqrt(pivots)
    half_scaled = (once * across).T * across
    gram_ref[...] = half_scaled + jnp.where(row == col, 0.0, half_scaled.T)
    done = eliminate([gram_ref[p : p + PANEL, :] for p in range(0, block, PANEL)], wide_ref, pair_ref)
    for p, panel in enumerate(done):
        factor_ref[p * PANEL : (p + 1) * PANEL, :] = panel
    factor = factor_ref[...] * (across * rows_total**0.5)
    moment = packed[half + 1 : half + 2] * (1.0 / rows_total)
    coefficients = jnp.sum(factor * moment, axis=1, keepdims=True)
    weights = jnp.sum(factor * coefficients, axis=0, keepdims=True)
    weights = split_rows(weights, 3)
    high = factor.astype(BF16)
    low = (factor - high.astype(F32)).astype(BF16)
    both = jnp.concatenate([high, low], axis=1)
    image = image_ref[...].reshape(blocks * block, block)
    basis = packed_ref[: blocks * block]
    new_image = dot(jnp.concatenate([image, image], axis=1), both, NT)
    new_image_ref[...] = new_image.astype(BF16).reshape(new_image_ref.shape)
    new_basis = dot(jnp.concatenate([basis, basis], axis=1), both, NT)
    new_ref[...] = new_basis.astype(BF16).reshape(new_ref.shape)
    guess = jnp.sum(dot(weights, basis, NT), axis=0, keepdims=True)
    fitted = jnp.sum(dot(weights, image, NT), axis=0, keepdims=True)
    for b in range(blocks):
        part = slice(b * block, (b + 1) * block)
        guess_ref[b : b + 1, :] = guess[:, part]
        residual_ref[b : b + 1, :] = rhs_ref[b : b + 1, :] - fitted[:, part]


def near(*arrays):
    return [pltpu.with_memory_space_constraint(array, pltpu.VMEM) for array in arrays]


def far(*arrays):
    return [pltpu.with_memory_space_constraint(array, pltpu.HBM) for array in arrays]


def vmem():
    return pl.BlockSpec(memory_space=pltpu.VMEM)


def smem():
    return pl.BlockSpec(memory_space=pltpu.SMEM)


def pack(basis, state):
    blocks, block, columns = basis.shape
    rows = blocks * block
    return pl.pallas_call(
        pack_kernel,
        out_shape=pltpu.VMEM((rows + 16 * pl.cdiv(blocks, 16), columns), BF16),
        in_specs=[pl.BlockSpec(memory_space=pl.ANY)] * 2,
        out_specs=vmem(),
        scratch_shapes=[pltpu.VMEM(state.shape, BF16), pltpu.SemaphoreType.DMA((PACK_COPIES + 1,))],
        compiler_params=pltpu.CompilerParams(vmem_limit_bytes=VMEM_LIMIT),
        name="pack",
    )(*far(basis.reshape(rows, columns), state))


def swap_pairs(parity, groups, devices):
    pairs = []
    for group in range(groups):
        for device in range(devices):
            other = device + 1 if device % 2 == parity else device - 1
            if 0 <= other < devices:
                pairs.append((group * devices + device, group * devices + other))
            else:
                twin = group ^ 1 if group ^ 1 < groups else group
                pairs.append((group * devices + device, twin * devices + device))
    return pairs


def halo(packed, basis, state):
    groups, devices = (lax.axis_size(axis) for axis in AXES)
    odd = lax.axis_index("dom") % 2
    got = []
    for parity in (1, 0):
        sent = packed
        if basis.shape[0] > HALO:
            up = odd == parity
            sent = pack(*(jnp.where(up, whole[-HALO:], whole[:HALO]) for whole in (basis, state)))
        got.append(lax.ppermute(sent, AXES, swap_pairs(parity, groups, devices)))
    return got


def exchange_stages(sizes):
    group, dom = sizes
    dom_bits = [1 << i for i in range(dom.bit_length() - 1)]
    group_bits = [dom << i for i in range(group.bit_length() - 1)]
    bits = group_bits[:1] + dom_bits[1:2] + dom_bits[2:] + group_bits[1:]
    stages = [dom_bits[:1], bits[:2] + [sum(bits[:2])], *([bit] for bit in bits[2:])]
    if len(dom_bits) < 2 or not group_bits:
        stages = [dom_bits[:1], *([bit] for bit in bits)]
    return stages[:1] + [[bit | 1 for bit in stage] for stage in stages[1:]]


def sum_parts(values):
    sizes = [lax.axis_size(axis) for axis in AXES]
    devices = sizes[0] * sizes[1]
    if any(size & (size - 1) for size in sizes):
        return [lax.psum(values, AXES)]
    parts = [values]
    for stage in exchange_stages(sizes):
        total = functools.reduce(jnp.add, parts)
        parts = [total]
        for bit in stage:
            pairs = [(i, i ^ bit) for i in range(devices)]
            parts.append(lax.ppermute(total, AXES, pairs))
    return parts


def finish(parts, image, packed, rhs, rows_total):
    blocks, block, columns = image.shape
    return pl.pallas_call(
        functools.partial(finish_kernel, rows_total=rows_total),
        out_shape=(
            jax.ShapeDtypeStruct(image.shape, BF16),
            jax.ShapeDtypeStruct(image.shape, BF16),
            jax.ShapeDtypeStruct(rhs.shape, F32),
            jax.ShapeDtypeStruct(rhs.shape, F32),
        ),
        in_specs=[vmem()] * (len(parts) + 3),
        out_specs=(vmem(),) * 4,
        scratch_shapes=[pltpu.VMEM((block, columns), F32)] * 2 + [pltpu.VMEM((2 * PANEL, columns), F32), pltpu.VMEM((2 * PANEL * PANEL, columns), F32)],
        compiler_params=pltpu.CompilerParams(vmem_limit_bytes=VMEM_LIMIT),
        name="finish",
    )(*near(*parts, image, packed, rhs))


def body(prior_basis, section_state, source, diag_blocks, coupling, neighbour_index, slot_count):
    blocks, block, columns = prior_basis.shape
    packed = pack(prior_basis, section_state)
    outer, inner = halo(packed, prior_basis, section_state)
    partial, base, near_coupling, *near_scalars = pl.pallas_call(
        local_kernel,
        out_shape=(
            pltpu.VMEM(prior_basis.shape, F32),
            pltpu.VMEM(source.shape, F32),
            pltpu.VMEM(coupling.shape, BF16),
            pltpu.SMEM(neighbour_index.shape, jnp.int32),
            pltpu.SMEM(slot_count.shape, jnp.int32),
            pltpu.SMEM((4,), jnp.int32),
        ),
        in_specs=[smem()] * 2 + [vmem()] * 3 + [pl.BlockSpec(memory_space=pl.ANY)],
        out_specs=(vmem(),) * 3 + (smem(),) * 3,
        scratch_shapes=[pltpu.SemaphoreType.DMA],
        compiler_params=pltpu.CompilerParams(vmem_limit_bytes=VMEM_LIMIT),
        name="local_part",
    )(*far(neighbour_index, slot_count), *near(packed), *far(source, diag_blocks, coupling))
    _, rhs, image, sums = pl.pallas_call(
        shared_kernel,
        out_shape=(
            pltpu.VMEM(prior_basis.shape, F32),
            pltpu.VMEM(source.shape, F32),
            pltpu.VMEM(prior_basis.shape, BF16),
            pltpu.VMEM((block // 2 + 8, columns), F32),
        ),
        in_specs=[smem()] * 3 + [vmem()] * 5,
        out_specs=(vmem(),) * 4,
        input_output_aliases={6: 0, 7: 1},
        compiler_params=pltpu.CompilerParams(vmem_limit_bytes=VMEM_LIMIT),
        name="shared_part",
    )(
        *(pltpu.with_memory_space_constraint(array, pltpu.SMEM) for array in near_scalars),
        *near(inner, outer, near_coupling, partial, base),
    )
    parts = sum_parts(sums)
    rows_total = blocks * block * lax.axis_size("group") * lax.axis_size("dom")
    return finish(parts, image, packed, rhs, float(rows_total))


def solution(mesh):
    rows = P(AXES, None)
    cubes = P(AXES, None, None)
    return jax.shard_map(
        body,
        mesh=mesh,
        in_specs=(cubes, rows, rows, cubes, P(AXES, None, None, None), rows, P(AXES)),
        out_specs=(cubes, cubes, rows, rows),
        check_vma=False,
    )
```
